32 devices in a mesh: gx: 2 (over core), gy: 4 (over z), gz: 4 (over y, x).
Axes of the slice: x: 2, y: 2, z: 4, core: 2. Of those that a mesh axis runs over, the one named last changes fastest.
Arguments:
- probe_vectors: float32 [32, 4, 32, 512], P(None, 'gx', 'gy', 'gz'), may hold values from -6 to 6
- layer_ids: int32 [4, 32, 512], P('gx', 'gy', 'gz'), may hold values from 0 to 15
- layer_kappa: float32 [16], replicated, may hold values from 0.1 to 10
- slot_order: int32 [8, 4], replicated, may hold values from 0 to 31, as said below
Outputs:
- factored: float32 [1024, 1024], P(('gx', 'gy'), 'gz')
The draws below stay inside these ranges and needn't reach their ends.
Inputs may be any that keep to these rules, and one draw needn't show every extreme that they name: `slot_order`: the entries are an ordering of 0 to 31, and in each column the entries divided by 4, rounded down, are an ordering of 0 to 7.
All inputs are finite; a program needn't handle non-finite values.
Results may differ from the reference program's by a relative error of at most 0.00013.
Values sent between devices are 32-bit elements; how exact they have to be, the bound alone decides.
A program may use at most 128 MiB of HBM per device.

```python
import math
import jax
import jax.numpy as jnp
from jax import lax

K = 32
CX = 2
CY = 8
CZ = 128
PASSES = 4
LAYERS = 16
NPAN = 2
NX = 4
NY = 32
NZ = 512
ORDER = 1024
PW = 128
N_GX = 2
N_GY = 4
N_GZ = 4
DEVICES = 32


def draw_slot_order(key, part):
    row_count = N_GX * N_GY
    group_key, place_key = jax.random.split(jax.random.fold_in(key, 11))
    group_keys = jax.random.split(group_key, N_GZ)
    place_keys = jax.random.split(place_key, row_count)
    groups = jax.vmap(lambda subkey: jax.random.permutation(subkey, row_count))(group_keys).T
    places = jax.vmap(lambda subkey: jax.random.permutation(subkey, N_GZ))(place_keys)
    columns = jnp.arange(N_GZ, dtype=jnp.int32)[None, :]
    position_in = places[groups, columns]
    return (groups * N_GZ + position_in).astype(jnp.int32)


def place_ends(array, key, low, high):
    longest = array.shape.index(max(array.shape))
    spots = []
    for shift in (0, 1):
        where = [jax.random.randint(jax.random.fold_in(key, axis), (), 0, length) for axis, length in enumerate(array.shape)]
        where[longest] = (where[longest] + shift) % array.shape[longest]
        spots.append(tuple(where))
    return array.at[spots[0]].set(low).at[spots[1]].set(high)


def level_of(stream_key, extent, shards, smallest, high):
    factor_of = 1.0
    for dim, parts in shards:
        heights = jax.random.uniform(jax.random.fold_in(jax.random.fold_in(stream_key, 6), dim), (parts,), jnp.float32, smallest / len(shards), high / len(shards))
        factor_of = factor_of * jnp.repeat(jnp.exp(heights), extent[dim] // parts).reshape((-1,) + (1,) * (len(extent) - 1 - dim))
    return factor_of


def normal_values(key, extent, deviation, bound, pieces=(), kind=jnp.bfloat16):
    result = jax.random.normal(key, extent, jnp.float32) * deviation
    if len(pieces) > 0:
        result = level_of(key, extent, pieces, -0.22, 0.18) * result
    return jnp.clip(result, min=-bound, max=bound).astype(kind)


def setup_inputs(seed: int = 0) -> dict:
    key_list = jax.random.split(jax.random.key(seed), 5)
    return {
        "probe_vectors": normal_values(key_list[0], (K, NX, NY, NZ), 1.0, 6.0, ((1, 2), (2, 4), (3, 4)), jnp.float32),
        "layer_ids": place_ends(jax.random.randint(key_list[1], (NX, NY, NZ), 0, LAYERS), jax.random.fold_in(key_list[1], 1), 0, LAYERS - 1).astype(jnp.int32),
        "layer_kappa": jnp.clip(jnp.exp(jax.random.uniform(key_list[2], (LAYERS,), jnp.float32, math.log(0.1), math.log(10.0))), 0.1, 10.0),
        "slot_order": draw_slot_order(jax.random.fold_in(key_list[4], 71), 0),
    }


upper_edge = 120.0
lower_edge = 24.0
coarse_shift = 1.0

def cheb_factors(step_index):
    center = (upper_edge + lower_edge) / (upper_edge - lower_edge)
    growth = math.log(center + math.sqrt(center * center - 1.0))

    def chebval(degree):
        expo = math.exp(degree * growth)
        return 0.5 * (expo + 1.0 / expo)
    if step_index == 0:
        return (1.0 / chebval(1), 0.0)
    return (2.0 * chebval(step_index) / chebval(step_index + 1), chebval(step_index - 1) / chebval(step_index + 1))

def face_weights(kappa_pad):
    center = kappa_pad[1:-1, 1:-1, 1:-1]
    x_plus = 0.5 * (center + kappa_pad[2:, 1:-1, 1:-1])
    x_minus = 0.5 * (center + kappa_pad[:-2, 1:-1, 1:-1])
    y_plus = 0.5 * (center + kappa_pad[1:-1, 2:, 1:-1])
    y_minus = 0.5 * (center + kappa_pad[1:-1, :-2, 1:-1])
    z_plus = 0.5 * (center + kappa_pad[1:-1, 1:-1, 2:])
    z_minus = 0.5 * (center + kappa_pad[1:-1, 1:-1, :-2])
    diagonal = x_plus + x_minus + y_plus + y_minus + z_plus + z_minus
    return ((x_plus, x_minus, y_plus, y_minus, z_plus, z_minus), diagonal)

def apply_operator(field_pad, weights, diagonal):
    x_plus, x_minus, y_plus, y_minus, z_plus, z_minus = weights
    interior = field_pad[..., 1:-1, 1:-1, 1:-1]
    beside = x_plus * field_pad[..., 2:, 1:-1, 1:-1] + x_minus * field_pad[..., :-2, 1:-1, 1:-1]
    beside = beside + y_plus * field_pad[..., 1:-1, 2:, 1:-1] + y_minus * field_pad[..., 1:-1, :-2, 1:-1]
    beside = beside + z_plus * field_pad[..., 1:-1, 1:-1, 2:] + z_minus * field_pad[..., 1:-1, 1:-1, :-2]
    return diagonal * interior - beside

def cheb_update(current, previous, applied, step_index):
    factor_one, factor_two = cheb_factors(step_index)
    shifted = (upper_edge + lower_edge) / (upper_edge - lower_edge) * current - 2.0 / (upper_edge - lower_edge) * applied
    return factor_one * shifted - factor_two * previous

def split_cells(values):
    return values.reshape(N_GX, CX, N_GY, CY, N_GZ, CZ)

def reference(probe_vectors, layer_ids, layer_kappa, slot_order):
    highest = lax.Precision.HIGHEST
    conductivity = layer_kappa[layer_ids]
    weights, diagonal = face_weights(jnp.pad(conductivity, 1))

    def filtered(vector):
        current = vector
        previous = jnp.zeros_like(vector)
        for step_index in range(PASSES):
            applied = apply_operator(jnp.pad(current, 1), weights, diagonal)
            current, previous = (cheb_update(current, previous, applied, step_index), current)
        return current
    basis = lax.map(filtered, probe_vectors)
    x_cell = jnp.arange(NX) % CX
    y_cell = jnp.arange(NY) % CY
    z_cell = jnp.arange(NZ) % CZ
    x_plus, x_minus, y_plus, y_minus, z_plus, z_minus = weights
    local_weights = (jnp.where((x_cell != CX - 1)[:, None, None], x_plus, 0.0), jnp.where((x_cell != 0)[:, None, None], x_minus, 0.0), jnp.where((y_cell != CY - 1)[None, :, None], y_plus, 0.0), jnp.where((y_cell != 0)[None, :, None], y_minus, 0.0), jnp.where((z_cell != CZ - 1)[None, None, :], z_plus, 0.0), jnp.where((z_cell != 0)[None, None, :], z_minus, 0.0))
    local_image = lax.map(lambda vector: apply_operator(jnp.pad(vector, 1), local_weights, diagonal), basis)
    scaling = 1.0 / math.sqrt(CX * CY * CZ)
    shaped = basis.reshape(K, N_GX, CX, N_GY, CY, N_GZ, CZ)
    shaped_image = local_image.reshape(K, N_GX, CX, N_GY, CY, N_GZ, CZ)
    self_blocks = scaling * jnp.einsum('kaxbycz,laxbycz->abckl', shaped, shaped_image, precision=highest)
    self_blocks = self_blocks + coarse_shift * jnp.eye(K, dtype=jnp.float32)
    x_block = -scaling * jnp.einsum('kabycz,abycz,labycz->abckl', shaped[:, :-1, CX - 1], split_cells(x_plus)[:-1, CX - 1], shaped[:, 1:, 0], precision=highest)
    y_block = -scaling * jnp.einsum('kaxbcz,axbcz,laxbcz->abckl', shaped[:, :, :, :-1, CY - 1], split_cells(y_plus)[:, :, :-1, CY - 1], shaped[:, :, :, 1:, 0], precision=highest)
    z_block = -scaling * jnp.einsum('kaxbyc,axbyc,laxbyc->abckl', shaped[:, :, :, :, :, :-1, CZ - 1], split_cells(z_plus)[:, :, :, :, :-1, CZ - 1], shaped[:, :, :, :, :, 1:, 0], precision=highest)
    position = slot_order.reshape(N_GX, N_GY, N_GZ).astype(jnp.int32)
    blocks = jnp.zeros((DEVICES, K, DEVICES, K), jnp.float32)
    flat_pos = position.ravel()
    blocks = blocks.at[flat_pos, :, flat_pos, :].set(self_blocks.reshape(-1, K, K))
    pairs = ((position[:-1].ravel(), position[1:].ravel(), x_block), (position[:, :-1].ravel(), position[:, 1:].ravel(), y_block), (position[:, :, :-1].ravel(), position[:, :, 1:].ravel(), z_block))
    for lower_pos, upper_pos, block_set in pairs:
        blocks = blocks.at[lower_pos, :, upper_pos, :].set(block_set.reshape(-1, K, K))
        blocks = blocks.at[upper_pos, :, lower_pos, :].set(jnp.swapaxes(block_set, -1, -2).reshape(-1, K, K))
    coarse = blocks.reshape(ORDER, ORDER)
    factored_cols = NPAN * PW
    factor_top = jnp.linalg.cholesky(coarse[:factored_cols, :factored_cols])
    below = jax.scipy.linalg.solve_triangular(factor_top, coarse[factored_cols:, :factored_cols].T, lower=True).T
    trailing = coarse[factored_cols:, factored_cols:] - jnp.dot(below, below.T, precision=highest)
    top_rows = jnp.concatenate([factor_top, jnp.zeros((factored_cols, ORDER - factored_cols), jnp.float32)], 1)
    return jnp.concatenate([top_rows, jnp.concatenate([below, trailing], 1)], 0)
```

```python
import functools
import math

import jax
import jax.numpy as jnp
from jax import lax
from jax.experimental import pallas as pl
from jax.experimental.pallas import tpu as pltpu
from jax.sharding import PartitionSpec as P

PASSES = 4
PANEL = 256
NPAN = 2
UPPER_EDGE = 120.0
LOWER_EDGE = 24.0
COARSE_SHIFT = 1.0
LANES = 128
MESH = pl.DeviceIdType.MESH
HIGHEST = lax.Precision.HIGHEST


def cheb_factors(step_index):
    center = (UPPER_EDGE + LOWER_EDGE) / (UPPER_EDGE - LOWER_EDGE)
    growth = math.log(center + math.sqrt(center * center - 1.0))

    def chebval(degree):
        expo = math.exp(degree * growth)
        return 0.5 * (expo + 1.0 / expo)

    if step_index == 0:
        return (1.0 / chebval(1), 0.0)
    return (
        2.0 * chebval(step_index) / chebval(step_index + 1),
        chebval(step_index - 1) / chebval(step_index + 1),
    )


def basis_kernel(
    counts, extents, vectors, layers,
    probe_ref, ids_ref, kappa_ref, out_ref,
    field, zsend, zrecv, weight, send_sem, recv_sem,
    line_send, line_recv, own_send, own_recv,
):
    nx, ny, nz = counts
    ex, ey, ez = extents
    groups = vectors // 8
    cells = ex * ey
    ix, iy, iz = lax.axis_index("gx"), lax.axis_index("gy"), lax.axis_index("gz")
    lines = (("gx", ix, nx), ("gy", iy, ny), ("gz", iz, nz))

    barrier = pltpu.get_barrier_semaphore()
    for axis, index, count in lines:
        for step in range(1, count):
            pl.semaphore_signal(
                barrier, inc=1, device_id={axis: lax.rem(index + step, count)}, device_id_type=MESH
            )

    lane = lax.broadcasted_iota(jnp.int32, (1, 8, ez), 2)
    zero_plane = jnp.zeros((groups + 1, 8, ez), jnp.float32)

    ids = ids_ref[...]
    kappa = jnp.zeros(ids.shape, jnp.float32)
    for layer in range(layers):
        kappa = jnp.where(ids == layer, kappa_ref[layer], kappa)
    for x in range(ex):
        for y in range(ey):
            k = x * ey + y
            field[0, x + 1, y + 1, 0:groups] = probe_ref[
                pl.ds(k, vectors, stride=cells), :
            ].reshape(groups, 8, ez)
            field[0, x + 1, y + 1, groups] = jnp.broadcast_to(kappa[k : k + 1, :], (8, ez))

    inside = (ix > 0, ix < nx - 1, iy > 0, iy < ny - 1, iz > 0, iz < nz - 1)

    def clear(side, phase):
        if side < 2:
            for y in range(ey):
                field[phase, 0 if side == 0 else ex + 1, y + 1] = zero_plane
        elif side < 4:
            for x in range(ex):
                field[phase, x + 1, 0 if side == 2 else ey + 1] = zero_plane
        else:
            zrecv[phase, side - 4] = zero_plane

    for side in range(6):
        @pl.when(jnp.logical_not(inside[side]))
        def _():
            for phase in range(PASSES + 1):
                clear(side, phase)

    def copy_of(phase, side):
        span = pl.ds(0, groups + 1 if phase == 0 else groups)
        axis, index, _ = lines[side // 2]
        low = side % 2 == 0
        target = index - 1 if low else index + 1
        if side < 2:
            src = field.at[phase, 1 if low else ex, pl.ds(1, ey), span]
            dst = field.at[phase, ex + 1 if low else 0, pl.ds(1, ey), span]
        elif side < 4:
            src = field.at[phase, pl.ds(1, ex), 1 if low else ey, span]
            dst = field.at[phase, pl.ds(1, ex), ey + 1 if low else 0, span]
        else:
            src = zsend.at[phase, 0 if low else 1, span]
            dst = zrecv.at[phase, 1 if low else 0, span]
        return pltpu.make_async_remote_copy(
            src_ref=src, dst_ref=dst,
            send_sem=send_sem.at[phase, side], recv_sem=recv_sem.at[phase, side],
            device_id={axis: target}, device_id_type=MESH,
        )

    def sides_of(phase):
        return range(6) if phase < PASSES else (0, 2, 4)

    def send(phase):
        span = groups + 1 if phase == 0 else groups
        for low in ((True, False) if phase < PASSES else (True,)):
            packed = jnp.zeros((span, 8, ez), jnp.float32)
            for x in range(ex):
                for y in range(ey):
                    k = x * ey + y
                    value = field[phase, x + 1, y + 1, 0:span]
                    shift = k if low else k + 1
                    if shift:
                        value = pltpu.roll(value, shift, 2)
                    packed = jnp.where(lane == k, value, packed)
            zsend[phase, 0 if low else 1, 0:span] = packed
        for side in sides_of(phase):
            @pl.when(inside[side])
            def _():
                copy_of(phase, side).start()

    def receive(phase):
        for side in sides_of(phase):
            @pl.when(inside[side ^ 1])
            def _():
                copy_of(phase, side).wait_recv()

    def z_neighbours(phase, k, value, part):
        span = value.shape[0]
        above = pltpu.roll(value, ez - 1, 2)
        ghost = zrecv[phase, 1, part : part + span]
        if (ez - 1 - k) % ez:
            ghost = pltpu.roll(ghost, ez - 1 - k, 2)
        above = jnp.where(lane == ez - 1, ghost, above)
        if phase == PASSES:
            return above, None
        below = pltpu.roll(value, 1, 2)
        ghost = zrecv[phase, 0, part : part + span]
        if k:
            ghost = pltpu.roll(ghost, ez - k, 2)
        return above, jnp.where(lane == 0, ghost, below)

    pl.semaphore_wait(barrier, sum(count - 1 for _, _, count in lines))

    for phase in range(PASSES):
        send(phase)
        receive(phase)
        if phase == 0:
            for x in range(1, ex + 1):
                for y in range(1, ey + 1):
                    k = (x - 1) * ey + y - 1
                    here = field[0, x, y, groups : groups + 1]
                    above, below = z_neighbours(0, k, here, groups)
                    beside = (
                        field[0, x + 1, y, groups : groups + 1], field[0, x - 1, y, groups : groups + 1],
                        field[0, x, y + 1, groups : groups + 1], field[0, x, y - 1, groups : groups + 1],
                        above, below,
                    )
                    total = None
                    for face in range(6):
                        value = 0.5 * (here + beside[face])
                        total = value if total is None else total + value
                        weight[face, k] = value[0]
                    weight[6, k] = total[0]
        factor_one, factor_two = cheb_factors(phase)
        shift = (UPPER_EDGE + LOWER_EDGE) / (UPPER_EDGE - LOWER_EDGE)
        slope = 2.0 / (UPPER_EDGE - LOWER_EDGE)
        for x in range(1, ex + 1):
            for y in range(1, ey + 1):
                k = (x - 1) * ey + y - 1
                here = field[phase, x, y, 0:groups]
                above, below = z_neighbours(phase, k, here, 0)
                beside = weight[0, k][None] * field[phase, x + 1, y, 0:groups]
                beside += weight[1, k][None] * field[phase, x - 1, y, 0:groups]
                beside += weight[2, k][None] * field[phase, x, y + 1, 0:groups]
                beside += weight[3, k][None] * field[phase, x, y - 1, 0:groups]
                beside += weight[4, k][None] * above + weight[5, k][None] * below
                applied = weight[6, k][None] * here - beside
                value = factor_one * (shift * here - slope * applied)
                if phase > 0:
                    value -= factor_two * field[phase - 1, x, y, 0:groups]
                field[phase + 1, x, y, 0:groups] = value

    send(PASSES)
    left, own = [], []
    for x in range(1, ex + 1):
        for y in range(1, ey + 1):
            k = (x - 1) * ey + y - 1
            here = field[PASSES, x, y, 0:groups]
            image = weight[6, k][None] * here
            if x < ex:
                image -= weight[0, k][None] * field[PASSES, x + 1, y, 0:groups]
            if x > 1:
                image -= weight[1, k][None] * field[PASSES, x - 1, y, 0:groups]
            if y < ey:
                image -= weight[2, k][None] * field[PASSES, x, y + 1, 0:groups]
            if y > 1:
                image -= weight[3, k][None] * field[PASSES, x, y - 1, 0:groups]
            above = jnp.where(lane == ez - 1, 0.0, pltpu.roll(here, ez - 1, 2))
            below = jnp.where(lane == 0, 0.0, pltpu.roll(here, 1, 2))
            image -= weight[4, k][None] * above + weight[5, k][None] * below
            left.append(here.reshape(vectors, ez))
            own.append(image.reshape(vectors, ez))
    receive(PASSES)
    right = []
    zeros = jnp.zeros((vectors, ez), jnp.float32)
    for x in range(1, ex + 1):
        for y in range(1, ey + 1):
            k = (x - 1) * ey + y - 1
            rows = [own[k], zeros, zeros]
            if x == ex:
                rows[1] = (-weight[0, k][None] * field[PASSES, x + 1, y, 0:groups]).reshape(vectors, ez)
            if y == ey:
                rows[2] = (-weight[2, k][None] * field[PASSES, x, y + 1, 0:groups]).reshape(vectors, ez)
            ghost = zrecv[PASSES, 1, 0:groups]
            if (ez - 1 - k) % ez:
                ghost = pltpu.roll(ghost, ez - 1 - k, 2)
            ghost = jnp.where(lane == ez - 1, -weight[4, k][None] * ghost, 0.0)
            rows.append(ghost.reshape(vectors, ez))
            right.append(jnp.concatenate(rows, axis=0))
    product = lax.dot_general(
        jnp.concatenate(left, axis=1), jnp.concatenate(right, axis=1),
        (((1,), (1,)), ((), ())), precision=HIGHEST, preferred_element_type=jnp.float32,
    ) * (1.0 / math.sqrt(cells * ez))
    row = lax.broadcasted_iota(jnp.int32, product.shape, 0)
    column = lax.broadcasted_iota(jnp.int32, product.shape, 1)
    out_ref[iz, ix, iy] = product + jnp.where(row == column, COARSE_SHIFT, 0.0)

    waits = []

    def spread(axis, index, count, ref_of, sends, recvs):
        copies = []
        for step in range(1, count):
            copy = pltpu.make_async_remote_copy(
                src_ref=ref_of(index), dst_ref=ref_of(index),
                send_sem=sends.at[step], recv_sem=recvs.at[step],
                device_id={axis: lax.rem(index + step, count)}, device_id_type=MESH,
            )
            copy.start()
            copies.append(copy)
        for step in range(1, count):
            source = ref_of(lax.rem(index + count - step, count))
            pltpu.make_async_remote_copy(
                src_ref=source, dst_ref=source,
                send_sem=sends.at[step], recv_sem=recvs.at[step],
                device_id={axis: lax.rem(index + step, count)}, device_id_type=MESH,
            ).wait_recv()
        waits.extend(copies)

    spread("gy", iy, ny, lambda i: out_ref.at[iz, ix, i], line_send.at[0], line_recv.at[0])
    spread("gz", iz, nz, lambda i: out_ref.at[i, ix], line_send.at[1], line_recv.at[1])
    spread("gx", ix, nx, lambda i: out_ref.at[:, i], line_send.at[2], line_recv.at[2])
    for copy in waits:
        copy.wait_send()
    for phase in range(PASSES + 1):
        for side in sides_of(phase):
            @pl.when(inside[side])
            def _():
                copy_of(phase, side).wait_send()


def factor_kernel(
    counts, vectors, width, rows_local, cols_local,
    slot_ref, blocks_ref, out_ref, place, panel, local, pivots,
):
    nx, ny, nz = counts
    ix, iy, iz = lax.axis_index("gx"), lax.axis_index("gy"), lax.axis_index("gz")
    rows_total = nx * ny
    row_block = (ix * ny + iy) * (rows_local // vectors)
    col_block = iz * (cols_local // vectors)
    wide = width // vectors
    per_tile = LANES // vectors

    def note(s, carry):
        place[slot_ref[s]] = s
        return carry

    lax.fori_loop(0, rows_total * nz, note, 0)
    panel[...] = jnp.zeros(panel.shape, jnp.float32)
    local[...] = jnp.zeros(local.shape, jnp.float32)
    lane = lax.broadcasted_iota(jnp.int32, (vectors, LANES), 1)

    def put(ref, row_at, col_at, value):
        rows = pl.ds(pl.multiple_of(row_at * vectors, vectors), vectors)
        cols = pl.ds(pl.multiple_of((col_at // per_tile) * LANES, LANES), LANES)
        ref[rows, cols] += pltpu.roll(value, (col_at % per_tile) * vectors, 1)

    def block_row(q, store):
        s = place[q]
        r, l = s // nz, s % nz
        i, j = r // ny, r % ny
        steps = ((ny, 0, i < nx - 1, i > 0), (1, 0, j < ny - 1, j > 0), (0, 1, l < nz - 1, l > 0))
        mine = blocks_ref[l, i, j]
        store(q, jnp.where(lane < vectors, mine, 0.0))
        for face, (dr, dl, up, down) in enumerate(steps):
            @pl.when(up)
            def _():
                value = pltpu.roll(mine, LANES - (face + 1) * vectors, 1)
                store(slot_ref[(r + dr) * nz + l + dl], jnp.where(lane < vectors, value, 0.0))

            @pl.when(down)
            def _():
                r2, l2 = r - dr, l - dl
                other = blocks_ref[l2, r2 // ny, r2 % ny]
                square = jnp.concatenate(
                    [other, jnp.zeros((LANES - vectors, LANES), jnp.float32)], axis=0
                )
                at = (face + 1) * vectors
                store(slot_ref[r2 * nz + l2], square.T[at : at + vectors, :])

    def top_row(q, carry):
        def store(c, value):
            pl.when(c < wide)(lambda: put(panel, q, c, value))
            pl.when((c >= col_block) & (c < col_block + cols_local // vectors))(
                lambda: put(panel, q, wide + c - col_block, value)
            )
            pl.when((c >= row_block) & (c < row_block + rows_local // vectors))(
                lambda: put(panel, q, wide + cols_local // vectors + c - row_block, value)
            )

        block_row(q, store)
        return carry

    def own_row(n, carry):
        def store(c, value):
            pl.when((c >= col_block) & (c < col_block + cols_local // vectors))(
                lambda: put(local, n, c - col_block, value)
            )

        block_row(row_block + n, store)
        return carry

    lax.fori_loop(0, wide, top_row, 0)
    lax.fori_loop(0, rows_local // vectors, own_row, 0)

    row8 = lax.broadcasted_iota(jnp.int32, (vectors, LANES), 0)

    def eliminate(b, carry):
        rows = pl.ds(pl.multiple_of(b * vectors, vectors), vectors)
        tile = pl.ds(pl.multiple_of((b // per_tile) * LANES, LANES), LANES)
        near = pltpu.roll(panel[rows, tile], (LANES - (b % per_tile) * vectors) % LANES, 1)
        body = panel[rows, :]
        pivot = jnp.ones((vectors, LANES), jnp.float32)
        inverse = jnp.ones((vectors, LANES), jnp.float32)
        for first in range(0, vectors, 8):
            columns = [
                jnp.broadcast_to(near[:, first + t : first + t + 1], (vectors, LANES)) for t in range(8)
            ]
            for t in range(8):
                j = first + t
                head = columns[t][j : j + 1, :]
                turn = 1.0 / head
                pivot = jnp.where(row8 == j, head, pivot)
                inverse = jnp.where(row8 == j, turn, inverse)
                factor = jnp.where(row8 > j, columns[t] * turn, 0.0)
                for u in range(t + 1, 8):
                    columns[u] = columns[u] - factor * columns[u][j : j + 1, :]
                near = near - factor * near[j : j + 1, :]
                spread = jnp.concatenate([factor] * (body.shape[1] // LANES), axis=1)
                body = body - spread * body[j : j + 1, :]
        panel[rows, :] = body
        pivots[rows, :] = pivot

        scaled = jnp.concatenate([inverse] * (width // LANES), axis=1) * body[:, :width]
        column = lax.broadcasted_iota(jnp.int32, scaled.shape, 1)
        scaled = jnp.where(column >= (b + 1) * vectors, scaled, 0.0)
        panel[...] -= jnp.dot(
            scaled.T, body, precision=HIGHEST, preferred_element_type=jnp.float32
        )
        return carry

    lax.fori_loop(0, wide, eliminate, 0)

    scale = lax.rsqrt(pivots[...])
    for tile in range(panel.shape[1] // LANES):
        if tile >= width // LANES:
            at = slice(tile * LANES, (tile + 1) * LANES)
            panel[:, at] = panel[:, at] * scale

    across = panel[:, width + cols_local :].T
    update = jnp.dot(
        across, panel[:, width : width + cols_local],
        precision=HIGHEST, preferred_element_type=jnp.float32,
    )
    row_ids = row_block * vectors + lax.broadcasted_iota(jnp.int32, (rows_local, LANES), 0)
    for tile in range(cols_local // LANES):
        at = slice(tile * LANES, (tile + 1) * LANES)
        start = iz * cols_local + tile * LANES
        col_ids = start + lax.broadcasted_iota(jnp.int32, (rows_local, LANES), 1)

        @pl.when(start < width)
        def _():
            part = panel[pl.ds(pl.multiple_of(start, LANES), LANES), width + cols_local :]
            out_ref[:, at] = jnp.where(col_ids <= row_ids, part.T, 0.0)

        @pl.when(start >= width)
        def _():
            rest = local[:, at] - update[:, at]
            out_ref[:, at] = jnp.where(row_ids >= width, rest, 0.0)


def on_device(probe_vectors, layer_ids, layer_kappa, slot_order):
    counts = tuple(lax.axis_size(axis) for axis in ("gx", "gy", "gz"))
    nx, ny, nz = counts
    vectors, ex, ey, ez = probe_vectors.shape
    layers = layer_kappa.shape[0]
    groups = vectors // 8
    vmem = pl.BlockSpec(memory_space=pltpu.VMEM)
    smem = pl.BlockSpec(memory_space=pltpu.SMEM)
    phases = PASSES + 1
    longest = max(counts)
    blocks = pl.pallas_call(
        functools.partial(basis_kernel, counts, (ex, ey, ez), vectors, layers),
        out_shape=jax.ShapeDtypeStruct((nz, nx, ny, vectors, LANES), jnp.float32),
        in_specs=[vmem, vmem, smem],
        out_specs=vmem,
        scratch_shapes=[
            pltpu.VMEM((phases, ex + 2, ey + 2, groups + 1, 8, ez), jnp.float32),
            pltpu.VMEM((phases, 2, groups + 1, 8, ez), jnp.float32),
            pltpu.VMEM((phases, 2, groups + 1, 8, ez), jnp.float32),
            pltpu.VMEM((7, ex * ey, 8, ez), jnp.float32),
            pltpu.SemaphoreType.DMA((phases, 6)),
            pltpu.SemaphoreType.DMA((phases, 6)),
            pltpu.SemaphoreType.DMA((3, longest)),
            pltpu.SemaphoreType.DMA((3, longest)),
            pltpu.SemaphoreType.DMA((longest,)),
            pltpu.SemaphoreType.DMA((longest,)),
        ],
        compiler_params=pltpu.CompilerParams(
            collective_id=0, has_side_effects=True, vmem_limit_bytes=48 * 1024 * 1024
        ),
        name="basis",
    )(probe_vectors.reshape(vectors * ex * ey, ez), layer_ids.reshape(ex * ey, ez), layer_kappa)

    rows_local, cols_local = nz * vectors, nx * ny * vectors
    width = NPAN * min(PANEL, rows_local, cols_local)
    return pl.pallas_call(
        functools.partial(factor_kernel, counts, vectors, width, rows_local, cols_local),
        out_shape=jax.ShapeDtypeStruct((rows_local, cols_local), jnp.float32),
        in_specs=[smem, vmem],
        out_specs=vmem,
        scratch_shapes=[
            pltpu.SMEM((nx * ny * nz,), jnp.int32),
            pltpu.VMEM((width, width + cols_local + rows_local), jnp.float32),
            pltpu.VMEM((rows_local, cols_local), jnp.float32),
            pltpu.VMEM((width, LANES), jnp.float32),
        ],
        compiler_params=pltpu.CompilerParams(vmem_limit_bytes=48 * 1024 * 1024),
        name="factor",
    )(slot_order.reshape(-1), blocks)


def solution(mesh):
    in_specs = (P(None, "gx", "gy", "gz"), P("gx", "gy", "gz"), P(), P())
    out_specs = P(("gx", "gy"), "gz")
    return jax.shard_map(
        on_device, mesh=mesh, in_specs=in_specs, out_specs=out_specs, check_vma=False
    )
```

```python
import functools
import math

import jax
import jax.numpy as jnp
from jax import lax
from jax.experimental import pallas as pl
from jax.experimental.pallas import tpu as pltpu
from jax.sharding import PartitionSpec as P

PASSES = 4
PANEL = 256
NPAN = 2
UPPER_EDGE = 120.0
LOWER_EDGE = 24.0
COARSE_SHIFT = 1.0
LANES = 128
MESH = pl.DeviceIdType.MESH
HIGHEST = lax.Precision.HIGHEST


def cheb_factors(step_index):
    center = (UPPER_EDGE + LOWER_EDGE) / (UPPER_EDGE - LOWER_EDGE)
    growth = math.log(center + math.sqrt(center * center - 1.0))

    def chebval(degree):
        expo = math.exp(degree * growth)
        return 0.5 * (expo + 1.0 / expo)

    if step_index == 0:
        return (1.0 / chebval(1), 0.0)
    return (
        2.0 * chebval(step_index) / chebval(step_index + 1),
        chebval(step_index - 1) / chebval(step_index + 1),
    )


def basis_kernel(
    counts, extents, vectors, layers,
    probe_ref, ids_ref, kappa_ref, out_ref,
    field, zsend, zrecv, weight, send_sem, recv_sem,
    line_send, line_recv, own_send, own_recv,
):
    nx, ny, nz = counts
    ex, ey, ez = extents
    groups = vectors // 8
    cells = ex * ey
    ix, iy, iz = lax.axis_index("gx"), lax.axis_index("gy"), lax.axis_index("gz")
    lines = (("gx", ix, nx), ("gy", iy, ny), ("gz", iz, nz))

    barrier = pltpu.get_barrier_semaphore()
    for axis, index, count in lines:
        for step in range(1, count):
            pl.semaphore_signal(
                barrier, inc=1, device_id={axis: lax.rem(index + step, count)}, device_id_type=MESH
            )

    lane = lax.broadcasted_iota(jnp.int32, (1, 8, ez), 2)
    zero_plane = jnp.zeros((groups + 1, 8, ez), jnp.float32)

    ids = ids_ref[...]
    kappa = jnp.zeros(ids.shape, jnp.float32)
    for layer in range(layers):
        kappa = jnp.where(ids == layer, kappa_ref[layer], kappa)
    for x in range(ex):
        for y in range(ey):
            k = x * ey + y
            field[0, x + 1, y + 1, 0:groups] = probe_ref[
                pl.ds(k, vectors, stride=cells), :
            ].reshape(groups, 8, ez)
            field[0, x + 1, y + 1, groups] = jnp.broadcast_to(kappa[k : k + 1, :], (8, ez))

    inside = (ix > 0, ix < nx - 1, iy > 0, iy < ny - 1, iz > 0, iz < nz - 1)

    def clear(side, phase):
        if side < 2:
            for y in range(ey):
                field[phase, 0 if side == 0 else ex + 1, y + 1] = zero_plane
        elif side < 4:
            for x in range(ex):
                field[phase, x + 1, 0 if side == 2 else ey + 1] = zero_plane
        else:
            zrecv[phase, side - 4] = zero_plane

    for side in range(6):
        @pl.when(jnp.logical_not(inside[side]))
        def _():
            for phase in range(PASSES + 1):
                clear(side, phase)

    def copy_of(phase, side):
        span = pl.ds(0, groups + 1 if phase == 0 else groups)
        axis, index, _ = lines[side // 2]
        low = side % 2 == 0
        target = index - 1 if low else index + 1
        if side < 2:
            src = field.at[phase, 1 if low else ex, pl.ds(1, ey), span]
            dst = field.at[phase, ex + 1 if low else 0, pl.ds(1, ey), span]
        elif side < 4:
            src = field.at[phase, pl.ds(1, ex), 1 if low else ey, span]
            dst = field.at[phase, pl.ds(1, ex), ey + 1 if low else 0, span]
        else:
            src = zsend.at[phase, 0 if low else 1, span]
            dst = zrecv.at[phase, 1 if low else 0, span]
        return pltpu.make_async_remote_copy(
            src_ref=src, dst_ref=dst,
            send_sem=send_sem.at[phase, side], recv_sem=recv_sem.at[phase, side],
            device_id={axis: target}, device_id_type=MESH,
        )

    def sides_of(phase):
        return range(6) if phase < PASSES else (0, 2, 4)

    def send(phase):
        span = groups + 1 if phase == 0 else groups
        for low in ((True, False) if phase < PASSES else (True,)):
            packed = jnp.zeros((span, 8, ez), jnp.float32)
            for x in range(ex):
                for y in range(ey):
                    k = x * ey + y
                    value = field[phase, x + 1, y + 1, 0:span]
                    shift = k if low else k + 1
                    if shift:
                        value = pltpu.roll(value, shift, 2)
                    packed = jnp.where(lane == k, value, packed)
            zsend[phase, 0 if low else 1, 0:span] = packed
        for side in sides_of(phase):
            @pl.when(inside[side])
            def _():
                copy_of(phase, side).start()

    def receive(phase):
        for side in sides_of(phase):
            @pl.when(inside[side ^ 1])
            def _():
                copy_of(phase, side).wait_recv()

    def z_neighbours(phase, k, value, part):
        span = value.shape[0]
        above = pltpu.roll(value, ez - 1, 2)
        ghost = zrecv[phase, 1, part : part + span]
        if (ez - 1 - k) % ez:
            ghost = pltpu.roll(ghost, ez - 1 - k, 2)
        above = jnp.where(lane == ez - 1, ghost, above)
        if phase == PASSES:
            return above, None
        below = pltpu.roll(value, 1, 2)
        ghost = zrecv[phase, 0, part : part + span]
        if k:
            ghost = pltpu.roll(ghost, ez - k, 2)
        return above, jnp.where(lane == 0, ghost, below)

    pl.semaphore_wait(barrier, sum(count - 1 for _, _, count in lines))

    for phase in range(PASSES):
        send(phase)
        receive(phase)
        if phase == 0:
            for x in range(1, ex + 1):
                for y in range(1, ey + 1):
                    k = (x - 1) * ey + y - 1
                    here = field[0, x, y, groups : groups + 1]
                    above, below = z_neighbours(0, k, here, groups)
                    beside = (
                        field[0, x + 1, y, groups : groups + 1], field[0, x - 1, y, groups : groups + 1],
                        field[0, x, y + 1, groups : groups + 1], field[0, x, y - 1, groups : groups + 1],
                        above, below,
                    )
                    total = None
                    for face in range(6):
                        value = 0.5 * (here + beside[face])
                        total = value if total is None else total + value
                        weight[face, k] = value[0]
                    weight[6, k] = total[0]
        factor_one, factor_two = cheb_factors(phase)
        shift = (UPPER_EDGE + LOWER_EDGE) / (UPPER_EDGE - LOWER_EDGE)
        slope = 2.0 / (UPPER_EDGE - LOWER_EDGE)
        for x in range(1, ex + 1):
            for y in range(1, ey + 1):
                k = (x - 1) * ey + y - 1
                here = field[phase, x, y, 0:groups]
                above, below = z_neighbours(phase, k, here, 0)
                beside = weight[0, k][None] * field[phase, x + 1, y, 0:groups]
                beside += weight[1, k][None] * field[phase, x - 1, y, 0:groups]
                beside += weight[2, k][None] * field[phase, x, y + 1, 0:groups]
                beside += weight[3, k][None] * field[phase, x, y - 1, 0:groups]
                beside += weight[4, k][None] * above + weight[5, k][None] * below
                applied = weight[6, k][None] * here - beside
                value = factor_one * (shift * here - slope * applied)
                if phase > 0:
                    value -= factor_two * field[phase - 1, x, y, 0:groups]
                field[phase + 1, x, y, 0:groups] = value

    send(PASSES)
    left, own = [], []
    for x in range(1, ex + 1):
        for y in range(1, ey + 1):
            k = (x - 1) * ey + y - 1
            here = field[PASSES, x, y, 0:groups]
            image = weight[6, k][None] * here
            if x < ex:
                image -= weight[0, k][None] * field[PASSES, x + 1, y, 0:groups]
            if x > 1:
                image -= weight[1, k][None] * field[PASSES, x - 1, y, 0:groups]
            if y < ey:
                image -= weight[2, k][None] * field[PASSES, x, y + 1, 0:groups]
            if y > 1:
                image -= weight[3, k][None] * field[PASSES, x, y - 1, 0:groups]
            above = jnp.where(lane == ez - 1, 0.0, pltpu.roll(here, ez - 1, 2))
            below = jnp.where(lane == 0, 0.0, pltpu.roll(here, 1, 2))
            image -= weight[4, k][None] * above + weight[5, k][None] * below
            left.append(here.reshape(vectors, ez))
            own.append(image.reshape(vectors, ez))
    receive(PASSES)
    right = []
    zeros = jnp.zeros((vectors, ez), jnp.float32)
    for x in range(1, ex + 1):
        for y in range(1, ey + 1):
            k = (x - 1) * ey + y - 1
            rows = [own[k], zeros, zeros]
            if x == ex:
                rows[1] = (-weight[0, k][None] * field[PASSES, x + 1, y, 0:groups]).reshape(vectors, ez)
            if y == ey:
                rows[2] = (-weight[2, k][None] * field[PASSES, x, y + 1, 0:groups]).reshape(vectors, ez)
            ghost = zrecv[PASSES, 1, 0:groups]
            if (ez - 1 - k) % ez:
                ghost = pltpu.roll(ghost, ez - 1 - k, 2)
            ghost = jnp.where(lane == ez - 1, -weight[4, k][None] * ghost, 0.0)
            rows.append(ghost.reshape(vectors, ez))
            right.append(jnp.concatenate(rows, axis=0))
    product = lax.dot_general(
        jnp.concatenate(left, axis=1), jnp.concatenate(right, axis=1),
        (((1,), (1,)), ((), ())), precision=HIGHEST, preferred_element_type=jnp.float32,
    ) * (1.0 / math.sqrt(cells * ez))
    row = lax.broadcasted_iota(jnp.int32, product.shape, 0)
    column = lax.broadcasted_iota(jnp.int32, product.shape, 1)
    out_ref[iz, ix, iy] = product + jnp.where(row == column, COARSE_SHIFT, 0.0)

    waits = []

    def spread(axis, index, count, ref_of, sends, recvs):
        copies = []
        for step in range(1, count):
            copy = pltpu.make_async_remote_copy(
                src_ref=ref_of(index), dst_ref=ref_of(index),
                send_sem=sends.at[step], recv_sem=recvs.at[step],
                device_id={axis: lax.rem(index + step, count)}, device_id_type=MESH,
            )
            copy.start()
            copies.append(copy)
        for step in range(1, count):
            source = ref_of(lax.rem(index + count - step, count))
            pltpu.make_async_remote_copy(
                src_ref=source, dst_ref=source,
                send_sem=sends.at[step], recv_sem=recvs.at[step],
                device_id={axis: lax.rem(index + step, count)}, device_id_type=MESH,
            ).wait_recv()
        waits.extend(copies)

    spread("gy", iy, ny, lambda i: out_ref.at[iz, ix, i], line_send.at[0], line_recv.at[0])
    spread("gz", iz, nz, lambda i: out_ref.at[i, ix], line_send.at[1], line_recv.at[1])
    spread("gx", ix, nx, lambda i: out_ref.at[:, i], line_send.at[2], line_recv.at[2])
    for copy in waits:
        copy.wait_send()
    for phase in range(PASSES + 1):
        for side in sides_of(phase):
            @pl.when(inside[side])
            def _():
                copy_of(phase, side).wait_send()


def split(value):
    high = value.astype(jnp.bfloat16)
    rest = value - high.astype(jnp.float32)
    middle = rest.astype(jnp.bfloat16)
    return high, middle, (rest - middle.astype(jnp.float32)).astype(jnp.bfloat16)


def left_stack(value):
    high, middle, low = split(value)
    return jnp.concatenate([high, high, middle, high, low, middle], axis=0)


def right_stack(value):
    high, middle, low = split(value)
    return jnp.concatenate([high, middle, high, low, high, middle], axis=0)


def factor_kernel(
    counts, vectors, width, rows_local, cols_local,
    slot_ref, blocks_ref, out_ref, place, strips, panel, local, across,
):
    nx, ny, nz = counts
    ix, iy, iz = lax.axis_index("gx"), lax.axis_index("gy"), lax.axis_index("gz")
    rows_total = nx * ny
    devices = rows_total * nz
    row_block = (ix * ny + iy) * (rows_local // vectors)
    wide = width // vectors
    per_tile = LANES // vectors
    own_cols = pl.ds(pl.multiple_of(iz * cols_local, LANES), cols_local)
    own_rows = pl.ds(pl.multiple_of(row_block * vectors, LANES), rows_local)

    def note(s, carry):
        place[slot_ref[s]] = s
        return carry

    lax.fori_loop(0, devices, note, 0, unroll=8)
    lane = lax.broadcasted_iota(jnp.int32, (vectors, LANES), 1)
    filler = jnp.zeros((LANES - 3 * vectors, LANES), jnp.float32)

    def block_row(q, at):
        strip = strips.at[at]
        strip[...] = jnp.zeros(strip.shape, jnp.float32)
        s = place[q]
        r, l = s // nz, s % nz
        i, j = r // ny, r % ny

        def put(c, value, lane_at):
            cols = pl.ds(pl.multiple_of((c // per_tile) * LANES, LANES), LANES)
            begin = (c % per_tile) * vectors
            moved = pltpu.roll(value, lax.rem(begin + LANES - lane_at, LANES), 1)
            pltpu.store(
                strip.at[:, cols], moved, mask=(lane >= begin) & (lane < begin + vectors)
            )

        mine = blocks_ref[l, i, j]
        put(q, mine, 0)
        faces = ((ny, 0, i < nx - 1, i > 0), (1, 0, j < ny - 1, j > 0), (0, 1, l < nz - 1, l > 0))
        below = []
        lower = []
        for face, (dr, dl, up, down) in enumerate(faces):
            n = jnp.where(up, s + dr * nz + dl, s)
            put(jnp.where(up, slot_ref[n], devices), mine, (face + 1) * vectors)
            n = jnp.where(down, s - dr * nz - dl, s)
            lower.append(jnp.where(down, slot_ref[n], devices))
            r2, l2 = n // nz, n % nz
            below.append(pltpu.roll(blocks_ref[l2, r2 // ny, r2 % ny], LANES - (face + 1) * vectors, 1))
        turned = jnp.concatenate(below + [filler], axis=0).T[:vectors, :]
        for face in range(3):
            put(lower[face], turned, face * vectors)
        return strip

    def top_row(q, carry):
        strip = block_row(q, q % 4)
        rows = pl.ds(pl.multiple_of(q * vectors, vectors), vectors)
        panel[rows, :width] = strip[:, :width]
        panel[rows, width : width + cols_local] = strip[:, own_cols]
        panel[rows, width + cols_local :] = strip[:, own_rows]
        return carry

    def own_row(n, carry):
        strip = block_row(row_block + n, n % 4)
        rows = pl.ds(pl.multiple_of(n * vectors, vectors), vectors)
        local[rows, :] = strip[:, own_cols]
        return carry

    lax.fori_loop(0, wide, top_row, 0, unroll=4)
    lax.fori_loop(0, rows_local // vectors, own_row, 0, unroll=4)

    row = lax.broadcasted_iota(jnp.int32, (8, LANES), 0)
    groups = vectors // 8

    def times(left, right):
        return lax.dot_general(
            left, right, (((0,), (0,)), ((), ())), preferred_element_type=jnp.float32
        )

    for b in range(wide):
        begin = (b // per_tile) * LANES
        lane_at = (b % per_tile) * vectors
        body = [panel[b * vectors + 8 * g : b * vectors + 8 * g + 8, begin:] for g in range(groups)]
        tiles = body[0].shape[1] // LANES
        pivots, inverses = [], []
        for g in range(groups):
            pivot = jnp.ones((8, LANES), jnp.float32)
            inverse = pivot
            columns = [
                [
                    jnp.broadcast_to(
                        body[h][:, lane_at + 8 * g + t : lane_at + 8 * g + t + 1], (8, LANES)
                    )
                    for h in range(g, groups)
                ]
                for t in range(8)
            ]
            for t in range(8):
                head = columns[t][0][t : t + 1, :]
                turn = 1.0 / head
                pivot = jnp.where(row == t, head, pivot)
                inverse = jnp.where(row == t, turn, inverse)
                kept = [jnp.where(row > t, columns[t][0], 0.0)] + columns[t][1:]
                for u in range(t + 1, 8):
                    across_row = columns[u][0][t : t + 1, :]
                    columns[u] = [
                        value - (part * across_row) * turn for value, part in zip(columns[u], kept)
                    ]
                body_row = body[g][t : t + 1, :]
                for h in range(g, groups):
                    factor = kept[h - g] * turn
                    body[h] = body[h] - jnp.concatenate([factor] * tiles, axis=1) * body_row
            pivots.append(pivot)
            inverses.append(inverse)
        strip = jnp.concatenate(body, axis=0)
        pivot = jnp.concatenate(pivots, axis=0)
        inverse = jnp.concatenate(inverses, axis=0)
        mine = strip[:, width + cols_local - begin :]
        across[b * vectors : (b + 1) * vectors, :] = mine * jnp.concatenate(
            [lax.rsqrt(pivot)] * (rows_local // LANES), axis=1
        )
        right = right_stack(strip)
        left_of = lambda value: left_stack(
            value * jnp.concatenate([inverse] * (value.shape[1] // LANES), axis=1)
        )
        for tile in range((b + 1) // per_tile, width // LANES):
            at = tile * LANES
            change = times(left_of(strip[:, at - begin : at - begin + LANES]), right[:, at - begin :])
            first = max((b + 1) * vectors, at)
            panel[first : at + LANES, at:] -= change[first - at :, :]
        local[...] -= times(left_of(mine), right[:, width - begin : width + cols_local - begin])

    row_ids = row_block * vectors + lax.broadcasted_iota(jnp.int32, (rows_local, LANES), 0)
    for tile in range(cols_local // LANES):
        at = slice(tile * LANES, (tile + 1) * LANES)
        start = iz * cols_local + tile * LANES
        col_ids = start + lax.broadcasted_iota(jnp.int32, (rows_local, LANES), 1)

        @pl.when(start < width)
        def _():
            part = across[pl.ds(pl.multiple_of(start, LANES), LANES), :]
            out_ref[:, at] = jnp.where(col_ids <= row_ids, part.T, 0.0)

        @pl.when(start >= width)
        def _():
            out_ref[:, at] = jnp.where(row_ids >= width, local[:, at], 0.0)


def on_device(probe_vectors, layer_ids, layer_kappa, slot_order):
    counts = tuple(lax.axis_size(axis) for axis in ("gx", "gy", "gz"))
    nx, ny, nz = counts
    vectors, ex, ey, ez = probe_vectors.shape
    layers = layer_kappa.shape[0]
    groups = vectors // 8
    vmem = pl.BlockSpec(memory_space=pltpu.VMEM)
    smem = pl.BlockSpec(memory_space=pltpu.SMEM)
    phases = PASSES + 1
    longest = max(counts)
    blocks = pl.pallas_call(
        functools.partial(basis_kernel, counts, (ex, ey, ez), vectors, layers),
        out_shape=jax.ShapeDtypeStruct((nz, nx, ny, vectors, LANES), jnp.float32),
        in_specs=[vmem, vmem, smem],
        out_specs=vmem,
        scratch_shapes=[
            pltpu.VMEM((phases, ex + 2, ey + 2, groups + 1, 8, ez), jnp.float32),
            pltpu.VMEM((phases, 2, groups + 1, 8, ez), jnp.float32),
            pltpu.VMEM((phases, 2, groups + 1, 8, ez), jnp.float32),
            pltpu.VMEM((7, ex * ey, 8, ez), jnp.float32),
            pltpu.SemaphoreType.DMA((phases, 6)),
            pltpu.SemaphoreType.DMA((phases, 6)),
            pltpu.SemaphoreType.DMA((3, longest)),
            pltpu.SemaphoreType.DMA((3, longest)),
            pltpu.SemaphoreType.DMA((longest,)),
            pltpu.SemaphoreType.DMA((longest,)),
        ],
        compiler_params=pltpu.CompilerParams(
            collective_id=0, has_side_effects=True, vmem_limit_bytes=48 * 1024 * 1024
        ),
        name="basis",
    )(probe_vectors.reshape(vectors * ex * ey, ez), layer_ids.reshape(ex * ey, ez), layer_kappa)

    rows_local, cols_local = nz * vectors, nx * ny * vectors
    width = NPAN * min(PANEL, rows_local, cols_local)
    return pl.pallas_call(
        functools.partial(factor_kernel, counts, vectors, width, rows_local, cols_local),
        out_shape=jax.ShapeDtypeStruct((rows_local, cols_local), jnp.float32),
        in_specs=[smem, vmem],
        out_specs=vmem,
        scratch_shapes=[
            pltpu.SMEM((nx * ny * nz,), jnp.int32),
            pltpu.VMEM((4, vectors, nx * ny * nz * vectors + LANES), jnp.float32),
            pltpu.VMEM((width, width + cols_local + rows_local), jnp.float32),
            pltpu.VMEM((rows_local, cols_local), jnp.float32),
            pltpu.VMEM((width, rows_local), jnp.float32),
        ],
        compiler_params=pltpu.CompilerParams(vmem_limit_bytes=48 * 1024 * 1024),
        name="factor",
    )(slot_order.reshape(-1), blocks)


def solution(mesh):
    in_specs = (P(None, "gx", "gy", "gz"), P("gx", "gy", "gz"), P(), P())
    out_specs = P(("gx", "gy"), "gz")
    return jax.shard_map(
        on_device, mesh=mesh, in_specs=in_specs, out_specs=out_specs, check_vma=False
    )
```

```python
import functools
import math

import jax
import jax.numpy as jnp
from jax import lax
from jax.experimental import pallas as pl
from jax.experimental.pallas import tpu as pltpu
from jax.sharding import PartitionSpec as P

PASSES = 4
PANEL = 256
NPAN = 2
UPPER_EDGE = 120.0
LOWER_EDGE = 24.0
COARSE_SHIFT = 1.0
LANES = 128
MESH = pl.DeviceIdType.MESH
HIGHEST = lax.Precision.HIGHEST


def cheb_factors(step_index):
    center = (UPPER_EDGE + LOWER_EDGE) / (UPPER_EDGE - LOWER_EDGE)
    growth = math.log(center + math.sqrt(center * center - 1.0))

    def chebval(degree):
        expo = math.exp(degree * growth)
        return 0.5 * (expo + 1.0 / expo)

    if step_index == 0:
        return (1.0 / chebval(1), 0.0)
    return (
        2.0 * chebval(step_index) / chebval(step_index + 1),
        chebval(step_index - 1) / chebval(step_index + 1),
    )


def basis_kernel(
    counts, extents, vectors, layers,
    probe_hbm, ids_hbm, kappa_hbm, out_ref,
    probe, ids, kappa_ref, field, zsend, zrecv, zghost, weight, weight_z,
    load_sem, send_sem, recv_sem, y_send, y_recv, z_send, z_recv, x_send, x_recv,
):
    nx, ny, nz = counts
    ex, ey, ez = extents
    groups = vectors // 8
    cells = ex * ey
    ix, iy, iz = lax.axis_index("gx"), lax.axis_index("gy"), lax.axis_index("gz")
    lines = (("gx", ix, nx), ("gy", iy, ny), ("gz", iz, nz))

    loads = [
        pltpu.make_async_copy(src, dst, load_sem.at[n])
        for n, (src, dst) in enumerate(((probe_hbm, probe), (ids_hbm, ids), (kappa_hbm, kappa_ref)))
    ]
    for load in loads:
        load.start()

    barrier = pltpu.get_barrier_semaphore()
    for axis, index, count in lines:
        for step in range(1, count):
            pl.semaphore_signal(
                barrier, inc=1, device_id={axis: lax.rem(index + step, count)}, device_id_type=MESH
            )

    lane = lax.broadcasted_iota(jnp.int32, (1, 8, ez), 2)
    even = lane % 2 == 0
    zero_plane = jnp.zeros((groups + 1, 8, ez), jnp.float32)
    inside = (ix > 0, ix < nx - 1, iy > 0, iy < ny - 1, iz > 0, iz < nz - 1)

    def clear(side, phase):
        if side < 2:
            for y in range(ey):
                field[phase, 0 if side == 0 else ex + 1, y + 1] = zero_plane
        elif side < 4:
            for x in range(ex):
                field[phase, x + 1, 0 if side == 2 else ey + 1] = zero_plane
        else:
            zrecv[phase, side - 4] = zero_plane

    for side in range(6):
        @pl.when(jnp.logical_not(inside[side]))
        def _():
            for phase in range(PASSES + 1):
                clear(side, phase)

    def number(x, y):
        return (x - 1) * ey + y - 1

    every = [(x, y) for y in range(1, ey + 1) for x in range(1, ex + 1)]
    order = [at for at in every if at[1] in (1, ey)] + [at for at in every if at[1] not in (1, ey)]
    edges = len([at for at in every if at[1] in (1, ey)])

    def copy_of(phase, side):
        span = pl.ds(0, groups + 1 if phase == 0 else groups)
        axis, index, _ = lines[side // 2]
        low = side % 2 == 0
        target = index - 1 if low else index + 1
        if side < 2:
            src = field.at[phase, 1 if low else ex, pl.ds(1, ey), span]
            dst = field.at[phase, ex + 1 if low else 0, pl.ds(1, ey), span]
        elif side < 4:
            src = field.at[phase, pl.ds(1, ex), 1 if low else ey, span]
            dst = field.at[phase, pl.ds(1, ex), ey + 1 if low else 0, span]
        else:
            src = zsend.at[phase, span]
            dst = zrecv.at[phase, 1 if low else 0, span]
        return pltpu.make_async_remote_copy(
            src_ref=src, dst_ref=dst,
            send_sem=send_sem.at[phase, side], recv_sem=recv_sem.at[phase, side],
            device_id={axis: target}, device_id_type=MESH,
        )

    def sides_of(phase, axis):
        return (2 * axis, 2 * axis + 1) if phase < PASSES else (2 * axis,)

    def send(phase, axis):
        for side in sides_of(phase, axis):
            @pl.when(inside[side])
            def _():
                copy_of(phase, side).start()

    def receive(phase, axis):
        for side in sides_of(phase, axis):
            @pl.when(inside[side ^ 1])
            def _():
                copy_of(phase, side).wait_recv()

    def packed(values, span):
        total = jnp.zeros((span, 8, ez), jnp.float32)
        for (x, y), value in values:
            k = number(x, y)
            turned = pltpu.roll(value, 2 * k, 2) if k else value
            total = jnp.where((lane == 2 * k) | (lane == (2 * k - 1) % ez), turned, total)
        return total

    def unpack(phase, span):
        above = pltpu.roll(zrecv[phase, 1, 0:span], ez - 1, 2)
        if phase == PASSES:
            return jnp.where(even, 0.0, above)
        return jnp.where(even, pltpu.roll(zrecv[phase, 0, 0:span], 1, 2), above)

    def ghost_of(value, k):
        return pltpu.roll(value, ez - 2 * k, 2) if k else value

    slope = 2.0 / (UPPER_EDGE - LOWER_EDGE)
    shift = (UPPER_EDGE + LOWER_EDGE) / (UPPER_EDGE - LOWER_EDGE)
    steps = ((1, 0), (-1, 0), (0, 1), (0, -1))

    def is_ghost(x, y, face):
        x2, y2 = x + steps[face][0], y + steps[face][1]
        return x2 in (0, ex + 1) or y2 in (0, ey + 1)

    def beside(phase, x, y, face):
        return field[phase, x + steps[face][0], y + steps[face][1], 0:groups]

    for load in loads:
        load.wait()
    for x, y in every:
        k = number(x, y)
        field[0, x, y, 0:groups] = probe[pl.ds(k, vectors, stride=cells), :].reshape(groups, 8, ez)
    for x in range(1, ex + 1):
        layer_of = ids[x - 1]
        kappa = jnp.zeros(layer_of.shape, jnp.float32)
        for layer in range(layers):
            kappa = jnp.where(layer_of == layer, kappa_ref[layer], kappa)
        for y in range(1, ey + 1):
            field[0, x, y, groups] = jnp.broadcast_to(kappa[y - 1 : y, :], (8, ez))

    pl.semaphore_wait(barrier, sum(count - 1 for _, _, count in lines))
    send(0, 1)
    zsend[0] = packed([((x, y), field[0, x, y]) for x, y in order], groups + 1)
    send(0, 2)
    send(0, 0)

    half = 0.5 * slope

    def kappa_at(x, y):
        return field[0, x, y, groups]

    def face_weight(x, y, face):
        weight[face, number(x, y)] = half * (
            kappa_at(x, y) + kappa_at(x + steps[face][0], y + steps[face][1])
        )

    flat = lane[0]
    for x, y in order:
        k = number(x, y)
        for face in range(4):
            if not is_ghost(x, y, face):
                face_weight(x, y, face)
        here = kappa_at(x, y)
        weight[4, k] = jnp.where(flat == ez - 1, 0.0, half * (here + pltpu.roll(here, ez - 1, 1)))
        weight[5, k] = jnp.where(flat == 0, 0.0, half * (here + pltpu.roll(here, 1, 1)))

    for phase in range(PASSES):
        factor_one, factor_two = cheb_factors(phase)
        for x, y in order:
            k = number(x, y)
            here = field[phase, x, y, 0:groups]
            value = shift * here
            for face in range(4):
                if not is_ghost(x, y, face):
                    value += weight[face, k][None] * (beside(phase, x, y, face) - here)
            value += weight[4, k][None] * (pltpu.roll(here, ez - 1, 2) - here)
            value += weight[5, k][None] * (pltpu.roll(here, 1, 2) - here)
            value = factor_one * value
            if phase > 0:
                value -= factor_two * field[phase - 1, x, y, 0:groups]
            field[phase + 1, x, y, 0:groups] = value
        for axis in range(3):
            receive(phase, axis)
        if phase == 0:
            ghosts = unpack(0, groups + 1)
            zsum = half * (zsend[0, groups] + ghosts[groups])
            weight_z[...] = jnp.where(even[0], 0.0, zsum)
            for x, y in order:
                k = number(x, y)
                for face in range(4):
                    if is_ghost(x, y, face):
                        face_weight(x, y, face)
                value = half * (kappa_at(x, y) + ghost_of(ghosts[groups:], k)[0])
                weight[6, k] = jnp.where((flat == 0) | (flat == ez - 1), value, 0.0)
        zghost[...] = unpack(phase, groups)
        done = []
        for n, (x, y) in enumerate(order):
            k = number(x, y)
            here = field[phase, x, y, 0:groups]
            value = weight[6, k][None] * (ghost_of(zghost[...], k) - here)
            for face in range(4):
                if is_ghost(x, y, face):
                    value += weight[face, k][None] * (beside(phase, x, y, face) - here)
            value = field[phase + 1, x, y, 0:groups] + factor_one * value
            field[phase + 1, x, y, 0:groups] = value
            if n == edges - 1:
                send(phase + 1, 1)
        zsend[phase + 1, 0:groups] = packed(
            [((x, y), field[phase + 1, x, y, 0:groups]) for x, y in order], groups
        )
        send(phase + 1, 2)
        send(phase + 1, 0)

    def product(left, right):
        return lax.dot_general(
            jnp.concatenate([value.reshape(vectors, ez) for value in left], axis=1),
            jnp.concatenate([value.reshape(vectors, ez) for value in right], axis=1),
            (((1,), (1,)), ((), ())), precision=HIGHEST, preferred_element_type=jnp.float32,
        )

    last = lambda x, y: field[PASSES, x, y, 0:groups]
    images = []
    for x, y in every:
        k = number(x, y)
        here = last(x, y)
        value = weight[6, k][None] * here
        for face in range(4):
            other = here if is_ghost(x, y, face) else here - beside(PASSES, x, y, face)
            value += weight[face, k][None] * other
        value += weight[4, k][None] * (here - pltpu.roll(here, ez - 1, 2))
        value += weight[5, k][None] * (here - pltpu.roll(here, 1, 2))
        images.append(value)
    scale = 1.0 / (slope * math.sqrt(cells * ez))
    own = scale * product([last(x, y) for x, y in every], images)
    row = lax.broadcasted_iota(jnp.int32, own.shape, 0)
    column = lax.broadcasted_iota(jnp.int32, own.shape, 1)
    own += jnp.where(row == column, COARSE_SHIFT, 0.0)

    for axis in range(3):
        receive(PASSES, axis)
    x_face = product(
        [last(ex, y) for y in range(1, ey + 1)],
        [weight[0, number(ex, y)][None] * beside(PASSES, ex, y, 0) for y in range(1, ey + 1)],
    )
    y_face = product(
        [last(x, ey) for x in range(1, ex + 1)],
        [weight[2, number(x, ey)][None] * beside(PASSES, x, ey, 2) for x in range(1, ex + 1)],
    )
    z_face = product([zsend[PASSES, 0:groups]], [weight_z[...][None] * unpack(PASSES, groups)])
    out_ref[iz, ix, iy] = jnp.concatenate(
        [own, -scale * x_face, -scale * y_face, -scale * z_face], axis=1
    )

    def spread(axis, index, count, source, sends, recvs, act):
        for step in range(1, count):
            chunk = out_ref.at[source]
            act(pltpu.make_async_remote_copy(
                src_ref=chunk, dst_ref=chunk, send_sem=sends(step), recv_sem=recvs(step),
                device_id={axis: lax.rem(index + step, count)}, device_id_type=MESH,
            ))

    def back(index, step, count):
        return lax.rem(index + count - step, count)

    def along_x(dz, dy, act):
        source = (back(iz, dz, nz), ix, back(iy, dy, ny))
        spread("gx", ix, nx, source, lambda step: x_send.at[step, dz, dy],
               lambda step: x_recv.at[step, dz, dy], act)

    def along_z(dy, act):
        source = (iz, ix, back(iy, dy, ny))
        spread("gz", iz, nz, source, lambda step: z_send.at[step, dy],
               lambda step: z_recv.at[step, dy], act)

    def along_y(act):
        spread("gy", iy, ny, (iz, ix, iy), lambda step: y_send.at[step],
               lambda step: y_recv.at[step], act)

    def arrived(source, send_at, recv_at, axis, index, count):
        chunk = out_ref.at[source]
        pltpu.make_async_remote_copy(
            src_ref=chunk, dst_ref=chunk, send_sem=send_at, recv_sem=recv_at,
            device_id={axis: lax.rem(index + 1, count)}, device_id_type=MESH,
        ).wait_recv()

    start = lambda copy: copy.start()
    along_y(start)
    along_z(0, start)
    along_x(0, 0, start)
    for dy in range(1, ny):
        arrived((iz, ix, back(iy, dy, ny)), y_send.at[dy], y_recv.at[dy], "gy", iy, ny)
        along_z(dy, start)
        along_x(0, dy, start)
    for dy in range(ny):
        for dz in range(1, nz):
            arrived((back(iz, dz, nz), ix, back(iy, dy, ny)), z_send.at[dz, dy], z_recv.at[dz, dy],
                    "gz", iz, nz)
            along_x(dz, dy, start)
    for dy in range(ny):
        for dz in range(nz):
            for dx in range(1, nx):
                arrived((back(iz, dz, nz), back(ix, dx, nx), back(iy, dy, ny)),
                        x_send.at[dx, dz, dy], x_recv.at[dx, dz, dy], "gx", ix, nx)

    finish = lambda copy: copy.wait_send()
    along_y(finish)
    for dy in range(ny):
        along_z(dy, finish)
        for dz in range(nz):
            along_x(dz, dy, finish)
    for phase in range(PASSES + 1):
        for axis in range(3):
            for side in sides_of(phase, axis):
                @pl.when(inside[side])
                def _():
                    copy_of(phase, side).wait_send()


def split(value):
    high = value.astype(jnp.bfloat16)
    rest = value - high.astype(jnp.float32)
    middle = rest.astype(jnp.bfloat16)
    return high, middle, (rest - middle.astype(jnp.float32)).astype(jnp.bfloat16)


def left_stack(value):
    high, middle, low = split(value)
    return jnp.concatenate([high, high, middle, high, low, middle], axis=0)


def right_stack(value):
    high, middle, low = split(value)
    return jnp.concatenate([high, middle, high, low, high, middle], axis=0)


def factor_kernel(
    counts, vectors, width, rows_local, cols_local,
    slot_ref, blocks_ref, out_ref, place, strips, panel, local, across,
):
    nx, ny, nz = counts
    ix, iy, iz = lax.axis_index("gx"), lax.axis_index("gy"), lax.axis_index("gz")
    rows_total = nx * ny
    devices = rows_total * nz
    row_block = (ix * ny + iy) * (rows_local // vectors)
    wide = width // vectors
    per_tile = LANES // vectors
    own_cols = pl.ds(pl.multiple_of(iz * cols_local, LANES), cols_local)
    own_rows = pl.ds(pl.multiple_of(row_block * vectors, LANES), rows_local)

    def note(s, carry):
        place[slot_ref[s]] = s
        return carry

    lax.fori_loop(0, devices, note, 0, unroll=8)
    lane = lax.broadcasted_iota(jnp.int32, (vectors, LANES), 1)
    filler = jnp.zeros((LANES - 3 * vectors, LANES), jnp.float32)

    def block_row(q, at):
        strip = strips.at[at]
        strip[...] = jnp.zeros(strip.shape, jnp.float32)
        s = place[q]
        r, l = s // nz, s % nz
        i, j = r // ny, r % ny

        def put(c, value, lane_at):
            cols = pl.ds(pl.multiple_of((c // per_tile) * LANES, LANES), LANES)
            begin = (c % per_tile) * vectors
            moved = pltpu.roll(value, lax.rem(begin + LANES - lane_at, LANES), 1)
            pltpu.store(
                strip.at[:, cols], moved, mask=(lane >= begin) & (lane < begin + vectors)
            )

        mine = blocks_ref[l, i, j]
        put(q, mine, 0)
        faces = ((ny, 0, i < nx - 1, i > 0), (1, 0, j < ny - 1, j > 0), (0, 1, l < nz - 1, l > 0))
        below = []
        lower = []
        for face, (dr, dl, up, down) in enumerate(faces):
            n = jnp.where(up, s + dr * nz + dl, s)
            put(jnp.where(up, slot_ref[n], devices), mine, (face + 1) * vectors)
            n = jnp.where(down, s - dr * nz - dl, s)
            lower.append(jnp.where(down, slot_ref[n], devices))
            r2, l2 = n // nz, n % nz
            below.append(pltpu.roll(blocks_ref[l2, r2 // ny, r2 % ny], LANES - (face + 1) * vectors, 1))
        turned = jnp.concatenate(below + [filler], axis=0).T[:vectors, :]
        for face in range(3):
            put(lower[face], turned, face * vectors)
        return strip

    def top_row(q, carry):
        strip = block_row(q, q % 4)
        rows = pl.ds(pl.multiple_of(q * vectors, vectors), vectors)
        panel[rows, :width] = strip[:, :width]
        panel[rows, width : width + cols_local] = strip[:, own_cols]
        panel[rows, width + cols_local :] = strip[:, own_rows]
        return carry

    def own_row(n, carry):
        strip = block_row(row_block + n, n % 4)
        rows = pl.ds(pl.multiple_of(n * vectors, vectors), vectors)
        local[rows, :] = strip[:, own_cols]
        return carry

    lax.fori_loop(0, wide, top_row, 0, unroll=4)
    lax.fori_loop(0, rows_local // vectors, own_row, 0, unroll=4)

    row = lax.broadcasted_iota(jnp.int32, (8, LANES), 0)
    groups = vectors // 8

    def times(left, right):
        return lax.dot_general(
            left, right, (((0,), (0,)), ((), ())), preferred_element_type=jnp.float32
        )

    for b in range(wide):
        begin = (b // per_tile) * LANES
        lane_at = (b % per_tile) * vectors
        body = [panel[b * vectors + 8 * g : b * vectors + 8 * g + 8, begin:] for g in range(groups)]
        tiles = body[0].shape[1] // LANES
        pivots, inverses = [], []
        for g in range(groups):
            pivot = jnp.ones((8, LANES), jnp.float32)
            inverse = pivot
            columns = [
                [
                    jnp.broadcast_to(
                        body[h][:, lane_at + 8 * g + t : lane_at + 8 * g + t + 1], (8, LANES)
                    )
                    for h in range(g, groups)
                ]
                for t in range(8)
            ]
            for t in range(8):
                head = columns[t][0][t : t + 1, :]
                turn = 1.0 / head
                pivot = jnp.where(row == t, head, pivot)
                inverse = jnp.where(row == t, turn, inverse)
                kept = [jnp.where(row > t, columns[t][0], 0.0)] + columns[t][1:]
                for u in range(t + 1, 8):
                    across_row = columns[u][0][t : t + 1, :]
                    columns[u] = [
                        value - (part * across_row) * turn for value, part in zip(columns[u], kept)
                    ]
                body_row = body[g][t : t + 1, :]
                for h in range(g, groups):
                    factor = kept[h - g] * turn
                    body[h] = body[h] - jnp.concatenate([factor] * tiles, axis=1) * body_row
            pivots.append(pivot)
            inverses.append(inverse)
        strip = jnp.concatenate(body, axis=0)
        pivot = jnp.concatenate(pivots, axis=0)
        inverse = jnp.concatenate(inverses, axis=0)
        mine = strip[:, width + cols_local - begin :]
        across[b * vectors : (b + 1) * vectors, :] = mine * jnp.concatenate(
            [lax.rsqrt(pivot)] * (rows_local // LANES), axis=1
        )
        right = right_stack(strip)
        left_of = lambda value: left_stack(
            value * jnp.concatenate([inverse] * (value.shape[1] // LANES), axis=1)
        )
        for tile in range((b + 1) // per_tile, width // LANES):
            at = tile * LANES
            change = times(left_of(strip[:, at - begin : at - begin + LANES]), right[:, at - begin :])
            first = max((b + 1) * vectors, at)
            panel[first : at + LANES, at:] -= change[first - at :, :]
        local[...] -= times(left_of(mine), right[:, width - begin : width + cols_local - begin])

    row_ids = row_block * vectors + lax.broadcasted_iota(jnp.int32, (rows_local, LANES), 0)
    for tile in range(cols_local // LANES):
        at = slice(tile * LANES, (tile + 1) * LANES)
        start = iz * cols_local + tile * LANES
        col_ids = start + lax.broadcasted_iota(jnp.int32, (rows_local, LANES), 1)

        @pl.when(start < width)
        def _():
            part = across[pl.ds(pl.multiple_of(start, LANES), LANES), :]
            out_ref[:, at] = jnp.where(col_ids <= row_ids, part.T, 0.0)

        @pl.when(start >= width)
        def _():
            out_ref[:, at] = jnp.where(row_ids >= width, local[:, at], 0.0)


def on_device(probe_vectors, layer_ids, layer_kappa, slot_order):
    counts = tuple(lax.axis_size(axis) for axis in ("gx", "gy", "gz"))
    nx, ny, nz = counts
    vectors, ex, ey, ez = probe_vectors.shape
    layers = layer_kappa.shape[0]
    groups = vectors // 8
    vmem = pl.BlockSpec(memory_space=pltpu.VMEM)
    smem = pl.BlockSpec(memory_space=pltpu.SMEM)
    anywhere = pl.BlockSpec(memory_space=pl.ANY)
    phases = PASSES + 1
    dma = pltpu.SemaphoreType.DMA
    blocks = pl.pallas_call(
        functools.partial(basis_kernel, counts, (ex, ey, ez), vectors, layers),
        out_shape=jax.ShapeDtypeStruct((nz, nx, ny, vectors, LANES), jnp.float32),
        in_specs=[anywhere] * 3,
        out_specs=vmem,
        scratch_shapes=[
            pltpu.VMEM((vectors * ex * ey, ez), jnp.float32),
            pltpu.VMEM((ex, ey, ez), jnp.int32),
            pltpu.SMEM((layers,), jnp.float32),
            pltpu.VMEM((phases, ex + 2, ey + 2, groups + 1, 8, ez), jnp.float32),
            pltpu.VMEM((phases, groups + 1, 8, ez), jnp.float32),
            pltpu.VMEM((phases, 2, groups + 1, 8, ez), jnp.float32),
            pltpu.VMEM((groups, 8, ez), jnp.float32),
            pltpu.VMEM((7, ex * ey, 8, ez), jnp.float32),
            pltpu.VMEM((8, ez), jnp.float32),
            dma((3,)), dma((phases, 6)), dma((phases, 6)),
            dma((ny,)), dma((ny,)), dma((nz, ny)), dma((nz, ny)), dma((nx, nz, ny)), dma((nx, nz, ny)),
        ],
        compiler_params=pltpu.CompilerParams(
            collective_id=0, has_side_effects=True, vmem_limit_bytes=48 * 1024 * 1024
        ),
        name="basis",
    )(probe_vectors.reshape(vectors * ex * ey, ez), layer_ids, layer_kappa)

    rows_local, cols_local = nz * vectors, nx * ny * vectors
    width = NPAN * min(PANEL, rows_local, cols_local)
    return pl.pallas_call(
        functools.partial(factor_kernel, counts, vectors, width, rows_local, cols_local),
        out_shape=jax.ShapeDtypeStruct((rows_local, cols_local), jnp.float32),
        in_specs=[smem, vmem],
        out_specs=vmem,
        scratch_shapes=[
            pltpu.SMEM((nx * ny * nz,), jnp.int32),
            pltpu.VMEM((4, vectors, nx * ny * nz * vectors + LANES), jnp.float32),
            pltpu.VMEM((width, width + cols_local + rows_local), jnp.float32),
            pltpu.VMEM((rows_local, cols_local), jnp.float32),
            pltpu.VMEM((width, rows_local), jnp.float32),
        ],
        compiler_params=pltpu.CompilerParams(vmem_limit_bytes=48 * 1024 * 1024),
        name="factor",
    )(slot_order.reshape(-1), blocks)


def solution(mesh):
    in_specs = (P(None, "gx", "gy", "gz"), P("gx", "gy", "gz"), P(), P())
    out_specs = P(("gx", "gy"), "gz")
    return jax.shard_map(
        on_device, mesh=mesh, in_specs=in_specs, out_specs=out_specs, check_vma=False
    )
```

```python
import functools
import math

import jax
import jax.numpy as jnp
from jax import lax
from jax.experimental import pallas as pl
from jax.experimental.pallas import tpu as pltpu
from jax.sharding import PartitionSpec as P

PASSES = 4
PANEL = 256
NPAN = 2
UPPER_EDGE = 120.0
LOWER_EDGE = 24.0
COARSE_SHIFT = 1.0
LANES = 128
MESH = pl.DeviceIdType.MESH


def cheb_factors(step_index):
    center = (UPPER_EDGE + LOWER_EDGE) / (UPPER_EDGE - LOWER_EDGE)
    growth = math.log(center + math.sqrt(center * center - 1.0))

    def chebval(degree):
        expo = math.exp(degree * growth)
        return 0.5 * (expo + 1.0 / expo)

    if step_index == 0:
        return (1.0 / chebval(1), 0.0)
    return (
        2.0 * chebval(step_index) / chebval(step_index + 1),
        chebval(step_index - 1) / chebval(step_index + 1),
    )


def basis_kernel(
    counts, extents, vectors, layers,
    probe_hbm, ids_hbm, kappa_hbm, out_ref,
    probe, ids, kappa_ref, field, zsend, zrecv, zghost, weight, weight_z,
    load_sem, send_sem, recv_sem, y_send, y_recv, z_send, z_recv, x_send, x_recv,
):
    nx, ny, nz = counts
    ex, ey, ez = extents
    groups = vectors // 8
    cells = ex * ey
    ix, iy, iz = lax.axis_index("gx"), lax.axis_index("gy"), lax.axis_index("gz")
    lines = (("gx", ix, nx), ("gy", iy, ny), ("gz", iz, nz))

    loads = [
        pltpu.make_async_copy(src, dst, load_sem.at[n])
        for n, (src, dst) in enumerate(((probe_hbm, probe), (ids_hbm, ids), (kappa_hbm, kappa_ref)))
    ]
    for load in loads:
        load.start()

    barrier = pltpu.get_barrier_semaphore()
    for axis, index, count in lines:
        for step in range(1, count):
            pl.semaphore_signal(
                barrier, inc=1, device_id={axis: lax.rem(index + step, count)}, device_id_type=MESH
            )

    lane = lax.broadcasted_iota(jnp.int32, (1, 8, ez), 2)
    even = lane % 2 == 0
    zero_plane = jnp.zeros((groups + 1, 8, ez), jnp.float32)
    inside = (ix > 0, ix < nx - 1, iy > 0, iy < ny - 1, iz > 0, iz < nz - 1)

    def clear(side, phase):
        if side < 2:
            for y in range(ey):
                field[phase, 0 if side == 0 else ex + 1, y + 1] = zero_plane
        elif side < 4:
            for x in range(ex):
                field[phase, x + 1, 0 if side == 2 else ey + 1] = zero_plane
        else:
            zrecv[phase, side - 4] = zero_plane

    for side in range(6):
        @pl.when(jnp.logical_not(inside[side]))
        def _():
            for phase in range(PASSES + 1):
                clear(side, phase)

    def number(x, y):
        return (x - 1) * ey + y - 1

    every = [(x, y) for y in range(1, ey + 1) for x in range(1, ex + 1)]
    order = [at for at in every if at[1] in (1, ey)] + [at for at in every if at[1] not in (1, ey)]
    edges = len([at for at in every if at[1] in (1, ey)])

    def copy_of(phase, side):
        span = pl.ds(0, groups + 1 if phase == 0 else groups)
        axis, index, _ = lines[side // 2]
        low = side % 2 == 0
        target = index - 1 if low else index + 1
        if side < 2:
            src = field.at[phase, 1 if low else ex, pl.ds(1, ey), span]
            dst = field.at[phase, ex + 1 if low else 0, pl.ds(1, ey), span]
        elif side < 4:
            src = field.at[phase, pl.ds(1, ex), 1 if low else ey, span]
            dst = field.at[phase, pl.ds(1, ex), ey + 1 if low else 0, span]
        else:
            src = zsend.at[phase, span]
            dst = zrecv.at[phase, 1 if low else 0, span]
        return pltpu.make_async_remote_copy(
            src_ref=src, dst_ref=dst,
            send_sem=send_sem.at[phase, side], recv_sem=recv_sem.at[phase, side],
            device_id={axis: target}, device_id_type=MESH,
        )

    def sides_of(phase, axis):
        return (2 * axis, 2 * axis + 1) if phase < PASSES else (2 * axis,)

    def send(phase, axis):
        for side in sides_of(phase, axis):
            @pl.when(inside[side])
            def _():
                copy_of(phase, side).start()

    def receive(phase, axis):
        for side in sides_of(phase, axis):
            @pl.when(inside[side ^ 1])
            def _():
                copy_of(phase, side).wait_recv()

    def packed(values, span):
        total = jnp.zeros((span, 8, ez), jnp.float32)
        for (x, y), value in values:
            k = number(x, y)
            turned = pltpu.roll(value, 2 * k, 2) if k else value
            total = jnp.where((lane == 2 * k) | (lane == (2 * k - 1) % ez), turned, total)
        return total

    def unpack(phase, span):
        above = pltpu.roll(zrecv[phase, 1, 0:span], ez - 1, 2)
        if phase == PASSES:
            return jnp.where(even, 0.0, above)
        return jnp.where(even, pltpu.roll(zrecv[phase, 0, 0:span], 1, 2), above)

    def ghost_of(value, k):
        return pltpu.roll(value, ez - 2 * k, 2) if k else value

    slope = 2.0 / (UPPER_EDGE - LOWER_EDGE)
    shift = (UPPER_EDGE + LOWER_EDGE) / (UPPER_EDGE - LOWER_EDGE)
    steps = ((1, 0), (-1, 0), (0, 1), (0, -1))

    def is_ghost(x, y, face):
        x2, y2 = x + steps[face][0], y + steps[face][1]
        return x2 in (0, ex + 1) or y2 in (0, ey + 1)

    def beside(phase, x, y, face):
        return field[phase, x + steps[face][0], y + steps[face][1], 0:groups]

    for load in loads:
        load.wait()
    for x, y in every:
        k = number(x, y)
        field[0, x, y, 0:groups] = probe[pl.ds(k, vectors, stride=cells), :].reshape(groups, 8, ez)
    for x in range(1, ex + 1):
        layer_of = ids[x - 1]
        kappa = jnp.zeros(layer_of.shape, jnp.float32)
        for layer in range(layers):
            kappa = jnp.where(layer_of == layer, kappa_ref[layer], kappa)
        for y in range(1, ey + 1):
            field[0, x, y, groups] = jnp.broadcast_to(kappa[y - 1 : y, :], (8, ez))

    pl.semaphore_wait(barrier, sum(count - 1 for _, _, count in lines))
    send(0, 1)
    zsend[0] = packed([((x, y), field[0, x, y]) for x, y in order], groups + 1)
    send(0, 2)
    send(0, 0)

    half = 0.5 * slope

    def kappa_at(x, y):
        return field[0, x, y, groups]

    def face_weight(x, y, face):
        weight[face, number(x, y)] = half * (
            kappa_at(x, y) + kappa_at(x + steps[face][0], y + steps[face][1])
        )

    flat = lane[0]
    for x, y in order:
        k = number(x, y)
        for face in range(4):
            if not is_ghost(x, y, face):
                face_weight(x, y, face)
        here = kappa_at(x, y)
        weight[4, k] = jnp.where(flat == ez - 1, 0.0, half * (here + pltpu.roll(here, ez - 1, 1)))
        weight[5, k] = jnp.where(flat == 0, 0.0, half * (here + pltpu.roll(here, 1, 1)))

    for phase in range(PASSES):
        factor_one, factor_two = cheb_factors(phase)
        for x, y in order:
            k = number(x, y)
            here = field[phase, x, y, 0:groups]
            value = shift * here
            for face in range(4):
                if not is_ghost(x, y, face):
                    value += weight[face, k][None] * (beside(phase, x, y, face) - here)
            value += weight[4, k][None] * (pltpu.roll(here, ez - 1, 2) - here)
            value += weight[5, k][None] * (pltpu.roll(here, 1, 2) - here)
            value = factor_one * value
            if phase > 0:
                value -= factor_two * field[phase - 1, x, y, 0:groups]
            field[phase + 1, x, y, 0:groups] = value
        for axis in range(3):
            receive(phase, axis)
        if phase == 0:
            ghosts = unpack(0, groups + 1)
            zsum = half * (zsend[0, groups] + ghosts[groups])
            weight_z[...] = jnp.where(even[0], 0.0, zsum)
            for x, y in order:
                k = number(x, y)
                for face in range(4):
                    if is_ghost(x, y, face):
                        face_weight(x, y, face)
                value = half * (kappa_at(x, y) + ghost_of(ghosts[groups:], k)[0])
                weight[6, k] = jnp.where((flat == 0) | (flat == ez - 1), value, 0.0)
        zghost[...] = unpack(phase, groups)
        done = []
        for n, (x, y) in enumerate(order):
            k = number(x, y)
            here = field[phase, x, y, 0:groups]
            value = weight[6, k][None] * (ghost_of(zghost[...], k) - here)
            for face in range(4):
                if is_ghost(x, y, face):
                    value += weight[face, k][None] * (beside(phase, x, y, face) - here)
            value = field[phase + 1, x, y, 0:groups] + factor_one * value
            field[phase + 1, x, y, 0:groups] = value
            if n == edges - 1:
                send(phase + 1, 1)
        send(phase + 1, 0)
        zsend[phase + 1, 0:groups] = packed(
            [((x, y), field[phase + 1, x, y, 0:groups]) for x, y in order], groups
        )
        send(phase + 1, 2)

    def product(left, right):
        left = jnp.concatenate(left, axis=1)
        right = jnp.concatenate(right, axis=1)
        left_high, right_high = left.astype(jnp.bfloat16), right.astype(jnp.bfloat16)
        left_low = (left - left_high.astype(jnp.float32)).astype(jnp.bfloat16)
        right_low = (right - right_high.astype(jnp.float32)).astype(jnp.bfloat16)
        return lax.dot_general(
            jnp.concatenate([left_high, left_high, left_low], axis=1),
            jnp.concatenate([right_high, right_low, right_high], axis=1),
            (((1,), (1,)), ((), ())), preferred_element_type=jnp.float32,
        )

    last = lambda x, y: field[PASSES, x, y, 0:groups].reshape(vectors, ez)
    images = []
    for x, y in every:
        k = number(x, y)
        here = field[PASSES, x, y, 0:groups]
        value = weight[6, k][None] * here
        for face in range(4):
            other = here if is_ghost(x, y, face) else here - beside(PASSES, x, y, face)
            value += weight[face, k][None] * other
        value += weight[4, k][None] * (here - pltpu.roll(here, ez - 1, 2))
        value += weight[5, k][None] * (here - pltpu.roll(here, 1, 2))
        images.append(value.reshape(vectors, ez))
    scale = 1.0 / (slope * math.sqrt(cells * ez))
    own = scale * product([last(x, y) for x, y in every], images)
    row = lax.broadcasted_iota(jnp.int32, own.shape, 0)
    column = lax.broadcasted_iota(jnp.int32, own.shape, 1)
    own += jnp.where(row == column, COARSE_SHIFT, 0.0)
    own = jnp.concatenate([own, jnp.zeros((vectors, LANES - vectors), jnp.float32)], axis=1)

    for axis in range(3):
        receive(PASSES, axis)
    zeros = jnp.zeros((vectors, ez), jnp.float32)

    def placed(value, face):
        rows = [zeros] * (LANES // vectors)
        rows[face + 1] = value.reshape(vectors, ez)
        return jnp.concatenate(rows, axis=0)

    left, right = [], []
    for y in range(1, ey + 1):
        left.append(last(ex, y))
        right.append(placed(weight[0, number(ex, y)][None] * beside(PASSES, ex, y, 0), 0))
    for x in range(1, ex + 1):
        left.append(last(x, ey))
        right.append(placed(weight[2, number(x, ey)][None] * beside(PASSES, x, ey, 2), 1))
    left.append(zsend[PASSES, 0:groups].reshape(vectors, ez))
    right.append(placed(weight_z[...][None] * unpack(PASSES, groups), 2))
    out_ref[iz, ix, iy] = own - scale * product(left, right)

    def spread(axis, index, count, source, sends, recvs, act):
        for step in range(1, count):
            chunk = out_ref.at[source]
            act(pltpu.make_async_remote_copy(
                src_ref=chunk, dst_ref=chunk, send_sem=sends(step), recv_sem=recvs(step),
                device_id={axis: lax.rem(index + step, count)}, device_id_type=MESH,
            ))

    def back(index, step, count):
        return lax.rem(index + count - step, count)

    def along_x(dz, dy, act):
        source = (back(iz, dz, nz), ix, back(iy, dy, ny))
        spread("gx", ix, nx, source, lambda step: x_send.at[step, dz, dy],
               lambda step: x_recv.at[step, dz, dy], act)

    def along_z(dy, act):
        source = (iz, ix, back(iy, dy, ny))
        spread("gz", iz, nz, source, lambda step: z_send.at[step, dy],
               lambda step: z_recv.at[step, dy], act)

    def along_y(act):
        spread("gy", iy, ny, (iz, ix, iy), lambda step: y_send.at[step],
               lambda step: y_recv.at[step], act)

    def arrived(source, send_at, recv_at, axis, index, count):
        chunk = out_ref.at[source]
        pltpu.make_async_remote_copy(
            src_ref=chunk, dst_ref=chunk, send_sem=send_at, recv_sem=recv_at,
            device_id={axis: lax.rem(index + 1, count)}, device_id_type=MESH,
        ).wait_recv()

    start = lambda copy: copy.start()
    along_y(start)
    along_z(0, start)
    along_x(0, 0, start)
    for dy in range(1, ny):
        arrived((iz, ix, back(iy, dy, ny)), y_send.at[dy], y_recv.at[dy], "gy", iy, ny)
        along_z(dy, start)
        along_x(0, dy, start)
    for dy in range(ny):
        for dz in range(1, nz):
            arrived((back(iz, dz, nz), ix, back(iy, dy, ny)), z_send.at[dz, dy], z_recv.at[dz, dy],
                    "gz", iz, nz)
            along_x(dz, dy, start)
    for dy in range(ny):
        for dz in range(nz):
            for dx in range(1, nx):
                arrived((back(iz, dz, nz), back(ix, dx, nx), back(iy, dy, ny)),
                        x_send.at[dx, dz, dy], x_recv.at[dx, dz, dy], "gx", ix, nx)

    finish = lambda copy: copy.wait_send()
    along_y(finish)
    for dy in range(ny):
        along_z(dy, finish)
        for dz in range(nz):
            along_x(dz, dy, finish)
    for phase in range(PASSES + 1):
        for axis in range(3):
            for side in sides_of(phase, axis):
                @pl.when(inside[side])
                def _():
                    copy_of(phase, side).wait_send()


def split(value):
    high = value.astype(jnp.bfloat16)
    rest = value - high.astype(jnp.float32)
    middle = rest.astype(jnp.bfloat16)
    return high, middle, (rest - middle.astype(jnp.float32)).astype(jnp.bfloat16)


def left_stack(value):
    high, middle, low = split(value)
    return jnp.concatenate([high, high, middle, high, low, middle], axis=0)


def right_stack(value):
    high, middle, low = split(value)
    return jnp.concatenate([high, middle, high, low, high, middle], axis=0)


def factor_kernel(
    counts, vectors, width, rows_local, cols_local,
    slot_hbm, blocks_ref, out_ref, slots, place, strips, panel, local, across, slot_sem,
):
    nx, ny, nz = counts
    ix, iy, iz = lax.axis_index("gx"), lax.axis_index("gy"), lax.axis_index("gz")
    rows_total = nx * ny
    devices = rows_total * nz
    row_block = (ix * ny + iy) * (rows_local // vectors)
    wide = width // vectors
    per_tile = LANES // vectors
    own_cols = pl.ds(pl.multiple_of(iz * cols_local, LANES), cols_local)
    own_rows = pl.ds(pl.multiple_of(row_block * vectors, LANES), rows_local)

    load = pltpu.make_async_copy(slot_hbm, slots, slot_sem)
    load.start()

    def slot_at(s):
        return slots[s % nz, s // nz]

    def note(s, carry):
        place[slot_at(s)] = s
        return carry

    load.wait()

    lax.fori_loop(0, devices, note, 0, unroll=8)
    lane = lax.broadcasted_iota(jnp.int32, (vectors, LANES), 1)
    filler = jnp.zeros((LANES - 3 * vectors, LANES), jnp.float32)

    def block_row(q, at):
        strip = strips.at[at]
        strip[...] = jnp.zeros(strip.shape, jnp.float32)
        s = place[q]
        r, l = s // nz, s % nz
        i, j = r // ny, r % ny

        def put(c, value, lane_at):
            cols = pl.ds(pl.multiple_of((c // per_tile) * LANES, LANES), LANES)
            begin = (c % per_tile) * vectors
            moved = pltpu.roll(value, lax.rem(begin + LANES - lane_at, LANES), 1)
            pltpu.store(
                strip.at[:, cols], moved, mask=(lane >= begin) & (lane < begin + vectors)
            )

        mine = blocks_ref[l, i, j]
        put(q, mine, 0)
        faces = ((ny, 0, i < nx - 1, i > 0), (1, 0, j < ny - 1, j > 0), (0, 1, l < nz - 1, l > 0))
        below = []
        lower = []
        for face, (dr, dl, up, down) in enumerate(faces):
            n = jnp.where(up, s + dr * nz + dl, s)
            put(jnp.where(up, slot_at(n), devices), mine, (face + 1) * vectors)
            n = jnp.where(down, s - dr * nz - dl, s)
            lower.append(jnp.where(down, slot_at(n), devices))
            r2, l2 = n // nz, n % nz
            below.append(pltpu.roll(blocks_ref[l2, r2 // ny, r2 % ny], LANES - (face + 1) * vectors, 1))
        turned = jnp.concatenate(below + [filler], axis=0).T[:vectors, :]
        for face in range(3):
            put(lower[face], turned, face * vectors)
        return strip

    def top_row(q, carry):
        strip = block_row(q, q % 4)
        rows = pl.ds(pl.multiple_of(q * vectors, vectors), vectors)
        panel[rows, :width] = strip[:, :width]
        panel[rows, width : width + cols_local] = strip[:, own_cols]
        panel[rows, width + cols_local :] = strip[:, own_rows]
        return carry

    def own_row(n, carry):
        strip = block_row(row_block + n, n % 4)
        rows = pl.ds(pl.multiple_of(n * vectors, vectors), vectors)
        local[rows, :] = strip[:, own_cols]
        return carry

    lax.fori_loop(0, wide, top_row, 0, unroll=4)
    lax.fori_loop(0, rows_local // vectors, own_row, 0, unroll=4)

    row = lax.broadcasted_iota(jnp.int32, (8, LANES), 0)
    groups = vectors // 8

    def times(left, right):
        return lax.dot_general(
            left, right, (((0,), (0,)), ((), ())), preferred_element_type=jnp.float32
        )

    for b in range(wide):
        begin = (b // per_tile) * LANES
        lane_at = (b % per_tile) * vectors
        body = [panel[b * vectors + 8 * g : b * vectors + 8 * g + 8, begin:] for g in range(groups)]
        tiles = body[0].shape[1] // LANES
        pivots, inverses = [], []
        for g in range(groups):
            pivot = jnp.ones((8, LANES), jnp.float32)
            inverse = pivot
            columns = [
                [
                    jnp.broadcast_to(
                        body[h][:, lane_at + 8 * g + t : lane_at + 8 * g + t + 1], (8, LANES)
                    )
                    for h in range(g, groups)
                ]
                for t in range(8)
            ]
            for t in range(8):
                head = columns[t][0][t : t + 1, :]
                turn = pl.reciprocal(head, approx=True)
                pivot = jnp.where(row == t, head, pivot)
                inverse = jnp.where(row == t, turn, inverse)
                kept = [jnp.where(row > t, columns[t][0], 0.0)] + columns[t][1:]
                for u in range(t + 1, 8):
                    across_row = columns[u][0][t : t + 1, :]
                    columns[u] = [
                        value - (part * across_row) * turn for value, part in zip(columns[u], kept)
                    ]
                body_row = body[g][t : t + 1, :]
                for h in range(g, groups):
                    factor = kept[h - g] * turn
                    body[h] = body[h] - jnp.concatenate([factor] * tiles, axis=1) * body_row
            pivots.append(pivot)
            inverses.append(inverse)
        strip = jnp.concatenate(body, axis=0)
        pivot = jnp.concatenate(pivots, axis=0)
        inverse = jnp.concatenate(inverses, axis=0)
        mine = strip[:, width + cols_local - begin :]
        across[b * vectors : (b + 1) * vectors, :] = mine * jnp.concatenate(
            [lax.rsqrt(pivot)] * (rows_local // LANES), axis=1
        )
        right = right_stack(strip)
        left_of = lambda value: left_stack(
            value * jnp.concatenate([inverse] * (value.shape[1] // LANES), axis=1)
        )
        for tile in range((b + 1) // per_tile, width // LANES):
            at = tile * LANES
            change = times(left_of(strip[:, at - begin : at - begin + LANES]), right[:, at - begin :])
            first = max((b + 1) * vectors, at)
            panel[first : at + LANES, at:] -= change[first - at :, :]
        local[...] -= times(left_of(mine), right[:, width - begin : width + cols_local - begin])

    row_ids = row_block * vectors + lax.broadcasted_iota(jnp.int32, (rows_local, LANES), 0)
    for tile in range(cols_local // LANES):
        at = slice(tile * LANES, (tile + 1) * LANES)
        start = iz * cols_local + tile * LANES
        col_ids = start + lax.broadcasted_iota(jnp.int32, (rows_local, LANES), 1)

        @pl.when(start < width)
        def _():
            part = across[pl.ds(pl.multiple_of(start, LANES), LANES), :]
            out_ref[:, at] = jnp.where(col_ids <= row_ids, part.T, 0.0)

        @pl.when(start >= width)
        def _():
            out_ref[:, at] = jnp.where(row_ids >= width, local[:, at], 0.0)


def on_device(probe_vectors, layer_ids, layer_kappa, slot_order):
    counts = tuple(lax.axis_size(axis) for axis in ("gx", "gy", "gz"))
    nx, ny, nz = counts
    vectors, ex, ey, ez = probe_vectors.shape
    layers = layer_kappa.shape[0]
    groups = vectors // 8
    vmem = pl.BlockSpec(memory_space=pltpu.VMEM)
    anywhere = pl.BlockSpec(memory_space=pltpu.HBM)
    phases = PASSES + 1
    dma = pltpu.SemaphoreType.DMA
    blocks = pl.pallas_call(
        functools.partial(basis_kernel, counts, (ex, ey, ez), vectors, layers),
        out_shape=jax.ShapeDtypeStruct((nz, nx, ny, vectors, LANES), jnp.float32),
        in_specs=[anywhere] * 3,
        out_specs=vmem,
        scratch_shapes=[
            pltpu.VMEM((vectors * ex * ey, ez), jnp.float32),
            pltpu.VMEM((ex, ey, ez), jnp.int32),
            pltpu.SMEM((layers,), jnp.float32),
            pltpu.VMEM((phases, ex + 2, ey + 2, groups + 1, 8, ez), jnp.float32),
            pltpu.VMEM((phases, groups + 1, 8, ez), jnp.float32),
            pltpu.VMEM((phases, 2, groups + 1, 8, ez), jnp.float32),
            pltpu.VMEM((groups, 8, ez), jnp.float32),
            pltpu.VMEM((7, ex * ey, 8, ez), jnp.float32),
            pltpu.VMEM((8, ez), jnp.float32),
            dma((3,)), dma((phases, 6)), dma((phases, 6)),
            dma((ny,)), dma((ny,)), dma((nz, ny)), dma((nz, ny)), dma((nx, nz, ny)), dma((nx, nz, ny)),
        ],
        compiler_params=pltpu.CompilerParams(
            collective_id=0, has_side_effects=True, vmem_limit_bytes=(64 * 1024 - 640) * 1024
        ),
        name="basis",
    )(probe_vectors.reshape(vectors * ex * ey, ez), layer_ids, layer_kappa)

    rows_local, cols_local = nz * vectors, nx * ny * vectors
    width = NPAN * min(PANEL, rows_local, cols_local)
    return pl.pallas_call(
        functools.partial(factor_kernel, counts, vectors, width, rows_local, cols_local),
        out_shape=jax.ShapeDtypeStruct((rows_local, cols_local), jnp.float32),
        in_specs=[anywhere, vmem],
        out_specs=vmem,
        scratch_shapes=[
            pltpu.SMEM((nz, nx * ny), jnp.int32),
            pltpu.SMEM((nx * ny * nz,), jnp.int32),
            pltpu.VMEM((4, vectors, nx * ny * nz * vectors + LANES), jnp.float32),
            pltpu.VMEM((width, width + cols_local + rows_local), jnp.float32),
            pltpu.VMEM((rows_local, cols_local), jnp.float32),
            pltpu.VMEM((width, rows_local), jnp.float32),
            dma(()),
        ],
        compiler_params=pltpu.CompilerParams(vmem_limit_bytes=48 * 1024 * 1024),
        name="factor",
    )(slot_order.T, blocks)


def solution(mesh):
    in_specs = (P(None, "gx", "gy", "gz"), P("gx", "gy", "gz"), P(), P())
    out_specs = P(("gx", "gy"), "gz")
    return jax.shard_map(
        on_device, mesh=mesh, in_specs=in_specs, out_specs=out_specs, check_vma=False
    )
```

```python
import functools
import math

import jax
import jax.numpy as jnp
from jax import lax
from jax.experimental import pallas as pl
from jax.experimental.pallas import tpu as pltpu
from jax.sharding import PartitionSpec as P

PASSES = 4
PANEL = 256
NPAN = 2
UPPER_EDGE = 120.0
LOWER_EDGE = 24.0
COARSE_SHIFT = 1.0
LANES = 128
MESH = pl.DeviceIdType.MESH


def cheb_factors(step_index):
    center = (UPPER_EDGE + LOWER_EDGE) / (UPPER_EDGE - LOWER_EDGE)
    growth = math.log(center + math.sqrt(center * center - 1.0))

    def chebval(degree):
        expo = math.exp(degree * growth)
        return 0.5 * (expo + 1.0 / expo)

    if step_index == 0:
        return (1.0 / chebval(1), 0.0)
    return (
        2.0 * chebval(step_index) / chebval(step_index + 1),
        chebval(step_index - 1) / chebval(step_index + 1),
    )


def basis_kernel(
    counts, extents, vectors, layers,
    probe_hbm, ids_hbm, kappa_hbm, out_ref,
    probe, ids, kappa_ref, field, zsend, zrecv, zghost, weight, weight_z,
    load_sem, send_sem, recv_sem, y_send, y_recv, z_send, z_recv, x_send, x_recv,
):
    nx, ny, nz = counts
    ex, ey, ez = extents
    groups = vectors // 8
    cells = ex * ey
    ix, iy, iz = lax.axis_index("gx"), lax.axis_index("gy"), lax.axis_index("gz")
    lines = (("gx", ix, nx), ("gy", iy, ny), ("gz", iz, nz))

    loads = [
        pltpu.make_async_copy(src, dst, load_sem.at[n])
        for n, (src, dst) in enumerate(((probe_hbm, probe), (ids_hbm, ids), (kappa_hbm, kappa_ref)))
    ]
    for load in loads:
        load.start()

    barrier = pltpu.get_barrier_semaphore()
    for axis, index, count in lines:
        for step in range(1, count):
            pl.semaphore_signal(
                barrier, inc=1, device_id={axis: lax.rem(index + step, count)}, device_id_type=MESH
            )

    lane = lax.broadcasted_iota(jnp.int32, (1, 8, ez), 2)
    even = lane % 2 == 0
    zero_plane = jnp.zeros((groups + 1, 8, ez), jnp.float32)
    inside = (ix > 0, ix < nx - 1, iy > 0, iy < ny - 1, iz > 0, iz < nz - 1)

    def clear(side, phase):
        if side < 2:
            for y in range(ey):
                field[phase, 0 if side == 0 else ex + 1, y + 1] = zero_plane
        elif side < 4:
            for x in range(ex):
                field[phase, x + 1, 0 if side == 2 else ey + 1] = zero_plane
        else:
            zrecv[phase, side - 4] = zero_plane

    for side in range(6):
        @pl.when(jnp.logical_not(inside[side]))
        def _():
            for phase in range(PASSES + 1):
                clear(side, phase)

    def number(x, y):
        return (x - 1) * ey + y - 1

    every = [(x, y) for y in range(1, ey + 1) for x in range(1, ex + 1)]
    order = [at for at in every if at[1] in (1, ey)] + [at for at in every if at[1] not in (1, ey)]
    edges = len([at for at in every if at[1] in (1, ey)])

    def copy_of(phase, side):
        span = pl.ds(0, groups + 1 if phase == 0 else groups)
        axis, index, _ = lines[side // 2]
        low = side % 2 == 0
        target = index - 1 if low else index + 1
        if side < 2:
            src = field.at[phase, 1 if low else ex, pl.ds(1, ey), span]
            dst = field.at[phase, ex + 1 if low else 0, pl.ds(1, ey), span]
        elif side < 4:
            src = field.at[phase, pl.ds(1, ex), 1 if low else ey, span]
            dst = field.at[phase, pl.ds(1, ex), ey + 1 if low else 0, span]
        else:
            src = zsend.at[phase, span]
            dst = zrecv.at[phase, 1 if low else 0, span]
        return pltpu.make_async_remote_copy(
            src_ref=src, dst_ref=dst,
            send_sem=send_sem.at[phase, side], recv_sem=recv_sem.at[phase, side],
            device_id={axis: target}, device_id_type=MESH,
        )

    def sides_of(phase, axis):
        return (2 * axis, 2 * axis + 1) if phase < PASSES else (2 * axis,)

    def send(phase, axis):
        for side in sides_of(phase, axis):
            @pl.when(inside[side])
            def _():
                copy_of(phase, side).start()

    def receive(phase, axis):
        for side in sides_of(phase, axis):
            @pl.when(inside[side ^ 1])
            def _():
                copy_of(phase, side).wait_recv()

    def packed(values, span):
        total = jnp.zeros((span, 8, ez), jnp.float32)
        for (x, y), value in values:
            k = number(x, y)
            turned = pltpu.roll(value, 2 * k, 2) if k else value
            total = jnp.where((lane == 2 * k) | (lane == (2 * k - 1) % ez), turned, total)
        return total

    def unpack(phase, span):
        above = pltpu.roll(zrecv[phase, 1, 0:span], ez - 1, 2)
        if phase == PASSES:
            return jnp.where(even, 0.0, above)
        return jnp.where(even, pltpu.roll(zrecv[phase, 0, 0:span], 1, 2), above)

    def ghost_of(value, k):
        return pltpu.roll(value, ez - 2 * k, 2) if k else value

    slope = 2.0 / (UPPER_EDGE - LOWER_EDGE)
    shift = (UPPER_EDGE + LOWER_EDGE) / (UPPER_EDGE - LOWER_EDGE)
    steps = ((1, 0), (-1, 0), (0, 1), (0, -1))

    def is_ghost(x, y, face):
        x2, y2 = x + steps[face][0], y + steps[face][1]
        return x2 in (0, ex + 1) or y2 in (0, ey + 1)

    def beside(phase, x, y, face):
        return field[phase, x + steps[face][0], y + steps[face][1], 0:groups]

    for load in loads:
        load.wait()
    for x, y in every:
        k = number(x, y)
        field[0, x, y, 0:groups] = probe[pl.ds(k, vectors, stride=cells), :].reshape(groups, 8, ez)
    for x in range(1, ex + 1):
        layer_of = ids[x - 1]
        kappa = jnp.zeros(layer_of.shape, jnp.float32)
        for layer in range(layers):
            kappa = jnp.where(layer_of == layer, kappa_ref[layer], kappa)
        for y in range(1, ey + 1):
            field[0, x, y, groups] = jnp.broadcast_to(kappa[y - 1 : y, :], (8, ez))

    pl.semaphore_wait(barrier, sum(count - 1 for _, _, count in lines))
    send(0, 1)
    zsend[0] = packed([((x, y), field[0, x, y]) for x, y in order], groups + 1)
    send(0, 2)
    send(0, 0)

    half = 0.5 * slope

    def kappa_at(x, y):
        return field[0, x, y, groups]

    def face_weight(x, y, face):
        weight[face, number(x, y)] = half * (
            kappa_at(x, y) + kappa_at(x + steps[face][0], y + steps[face][1])
        )

    flat = lane[0]
    for x, y in order:
        k = number(x, y)
        for face in range(4):
            if not is_ghost(x, y, face):
                face_weight(x, y, face)
        here = kappa_at(x, y)
        weight[4, k] = jnp.where(flat == ez - 1, 0.0, half * (here + pltpu.roll(here, ez - 1, 1)))
        weight[5, k] = jnp.where(flat == 0, 0.0, half * (here + pltpu.roll(here, 1, 1)))

    for phase in range(PASSES):
        factor_one, factor_two = cheb_factors(phase)
        for x, y in order:
            k = number(x, y)
            here = field[phase, x, y, 0:groups]
            value = shift * here
            for face in range(4):
                if not is_ghost(x, y, face):
                    value += weight[face, k][None] * (beside(phase, x, y, face) - here)
            value += weight[4, k][None] * (pltpu.roll(here, ez - 1, 2) - here)
            value += weight[5, k][None] * (pltpu.roll(here, 1, 2) - here)
            value = factor_one * value
            if phase > 0:
                value -= factor_two * field[phase - 1, x, y, 0:groups]
            field[phase + 1, x, y, 0:groups] = value
        for axis in range(3):
            receive(phase, axis)
        if phase == 0:
            ghosts = unpack(0, groups + 1)
            zsum = half * (zsend[0, groups] + ghosts[groups])
            weight_z[...] = jnp.where(even[0], 0.0, zsum)
            for x, y in order:
                k = number(x, y)
                for face in range(4):
                    if is_ghost(x, y, face):
                        face_weight(x, y, face)
                value = half * (kappa_at(x, y) + ghost_of(ghosts[groups:], k)[0])
                weight[6, k] = jnp.where((flat == 0) | (flat == ez - 1), value, 0.0)
        zghost[...] = unpack(phase, groups)
        done = []
        for n, (x, y) in enumerate(order):
            k = number(x, y)
            here = field[phase, x, y, 0:groups]
            value = weight[6, k][None] * (ghost_of(zghost[...], k) - here)
            for face in range(4):
                if is_ghost(x, y, face):
                    value += weight[face, k][None] * (beside(phase, x, y, face) - here)
            value = field[phase + 1, x, y, 0:groups] + factor_one * value
            field[phase + 1, x, y, 0:groups] = value
            if n == edges - 1:
                send(phase + 1, 1)
        send(phase + 1, 0)
        zsend[phase + 1, 0:groups] = packed(
            [((x, y), field[phase + 1, x, y, 0:groups]) for x, y in order], groups
        )
        send(phase + 1, 2)

    def product(left, right):
        left = jnp.concatenate(left, axis=1)
        right = jnp.concatenate(right, axis=1)
        left_high, right_high = left.astype(jnp.bfloat16), right.astype(jnp.bfloat16)
        left_low = (left - left_high.astype(jnp.float32)).astype(jnp.bfloat16)
        right_low = (right - right_high.astype(jnp.float32)).astype(jnp.bfloat16)
        return lax.dot_general(
            jnp.concatenate([left_high, left_high, left_low], axis=1),
            jnp.concatenate([right_high, right_low, right_high], axis=1),
            (((1,), (1,)), ((), ())), preferred_element_type=jnp.float32,
        )

    last = lambda x, y: field[PASSES, x, y, 0:groups].reshape(vectors, ez)
    images = []
    for x, y in every:
        k = number(x, y)
        here = field[PASSES, x, y, 0:groups]
        value = weight[6, k][None] * here
        for face in range(4):
            other = here if is_ghost(x, y, face) else here - beside(PASSES, x, y, face)
            value += weight[face, k][None] * other
        value += weight[4, k][None] * (here - pltpu.roll(here, ez - 1, 2))
        value += weight[5, k][None] * (here - pltpu.roll(here, 1, 2))
        images.append(value.reshape(vectors, ez))
    scale = 1.0 / (slope * math.sqrt(cells * ez))
    own = scale * product([last(x, y) for x, y in every], images)
    row = lax.broadcasted_iota(jnp.int32, own.shape, 0)
    column = lax.broadcasted_iota(jnp.int32, own.shape, 1)
    own += jnp.where(row == column, COARSE_SHIFT, 0.0)
    own = jnp.concatenate([own, jnp.zeros((vectors, LANES - vectors), jnp.float32)], axis=1)

    for axis in range(3):
        receive(PASSES, axis)
    zeros = jnp.zeros((vectors, ez), jnp.float32)

    def placed(value, face):
        rows = [zeros] * (LANES // vectors)
        rows[face + 1] = value.reshape(vectors, ez)
        return jnp.concatenate(rows, axis=0)

    left, right = [], []
    for y in range(1, ey + 1):
        left.append(last(ex, y))
        right.append(placed(weight[0, number(ex, y)][None] * beside(PASSES, ex, y, 0), 0))
    for x in range(1, ex + 1):
        left.append(last(x, ey))
        right.append(placed(weight[2, number(x, ey)][None] * beside(PASSES, x, ey, 2), 1))
    left.append(zsend[PASSES, 0:groups].reshape(vectors, ez))
    right.append(placed(weight_z[...][None] * unpack(PASSES, groups), 2))
    out_ref[iz, ix, iy] = own - scale * product(left, right)

    def spread(axis, index, count, source, sends, recvs, act):
        for step in range(1, count):
            chunk = out_ref.at[source]
            act(pltpu.make_async_remote_copy(
                src_ref=chunk, dst_ref=chunk, send_sem=sends(step), recv_sem=recvs(step),
                device_id={axis: lax.rem(index + step, count)}, device_id_type=MESH,
            ))

    def back(index, step, count):
        return lax.rem(index + count - step, count)

    def along_x(dz, dy, act):
        source = (back(iz, dz, nz), ix, back(iy, dy, ny))
        spread("gx", ix, nx, source, lambda step: x_send.at[step, dz, dy],
               lambda step: x_recv.at[step, dz, dy], act)

    def along_z(dy, act):
        source = (iz, ix, back(iy, dy, ny))
        spread("gz", iz, nz, source, lambda step: z_send.at[step, dy],
               lambda step: z_recv.at[step, dy], act)

    def along_y(act):
        spread("gy", iy, ny, (iz, ix, iy), lambda step: y_send.at[step],
               lambda step: y_recv.at[step], act)

    def arrived(source, send_at, recv_at, axis, index, count):
        chunk = out_ref.at[source]
        pltpu.make_async_remote_copy(
            src_ref=chunk, dst_ref=chunk, send_sem=send_at, recv_sem=recv_at,
            device_id={axis: lax.rem(index + 1, count)}, device_id_type=MESH,
        ).wait_recv()

    start = lambda copy: copy.start()
    along_y(start)
    along_z(0, start)
    along_x(0, 0, start)
    for dy in range(1, ny):
        arrived((iz, ix, back(iy, dy, ny)), y_send.at[dy], y_recv.at[dy], "gy", iy, ny)
        along_z(dy, start)
        along_x(0, dy, start)
    for dy in range(ny):
        for dz in range(1, nz):
            arrived((back(iz, dz, nz), ix, back(iy, dy, ny)), z_send.at[dz, dy], z_recv.at[dz, dy],
                    "gz", iz, nz)
            along_x(dz, dy, start)
    for dy in range(ny):
        for dz in range(nz):
            for dx in range(1, nx):
                arrived((back(iz, dz, nz), back(ix, dx, nx), back(iy, dy, ny)),
                        x_send.at[dx, dz, dy], x_recv.at[dx, dz, dy], "gx", ix, nx)

    finish = lambda copy: copy.wait_send()
    along_y(finish)
    for dy in range(ny):
        along_z(dy, finish)
        for dz in range(nz):
            along_x(dz, dy, finish)
    for phase in range(PASSES + 1):
        for axis in range(3):
            for side in sides_of(phase, axis):
                @pl.when(inside[side])
                def _():
                    copy_of(phase, side).wait_send()


def split(value):
    high = value.astype(jnp.bfloat16)
    rest = value - high.astype(jnp.float32)
    middle = rest.astype(jnp.bfloat16)
    return high, middle, (rest - middle.astype(jnp.float32)).astype(jnp.bfloat16)


def left_stack(value):
    high, middle, low = split(value)
    return jnp.concatenate([high, high, middle, high, low, middle], axis=0)


def right_stack(value):
    high, middle, low = split(value)
    return jnp.concatenate([high, middle, high, low, high, middle], axis=0)


def factor_kernel(
    counts, vectors, width, rows_local, cols_local,
    slot_hbm, blocks_ref, out_ref, slots, place, panel, local, across, slot_sem,
):
    nx, ny, nz = counts
    ix, iy, iz = lax.axis_index("gx"), lax.axis_index("gy"), lax.axis_index("gz")
    rows_total = nx * ny
    devices = rows_total * nz
    row_block = (ix * ny + iy) * (rows_local // vectors)
    wide = width // vectors
    per_tile = LANES // vectors
    col_block = iz * (cols_local // vectors)

    load = pltpu.make_async_copy(slot_hbm, slots, slot_sem)
    load.start()
    panel[...] = jnp.zeros(panel.shape, jnp.float32)
    local[...] = jnp.zeros(local.shape, jnp.float32)

    def slot_at(s):
        return slots[s % nz, s // nz]

    def note(s, carry):
        place[slot_at(s)] = s
        return carry

    load.wait()

    lax.fori_loop(0, devices, note, 0, unroll=8)
    lane = lax.broadcasted_iota(jnp.int32, (vectors, LANES), 1)
    filler = jnp.zeros((LANES - 3 * vectors, LANES), jnp.float32)
    nowhere = 4 * devices
    own_cols = (col_block, cols_local // vectors)
    own_rows = (row_block, rows_local // vectors)

    def block_row(q, ref, at, targets):
        rows = pl.ds(pl.multiple_of(at * vectors, vectors), vectors)
        s = place[q]
        r, l = s // nz, s % nz
        i, j = r // ny, r % ny

        def put(c, value, lane_at):
            begin = (c % per_tile) * vectors
            moved = pltpu.roll(value, lax.rem(begin + LANES - lane_at, LANES), 1)
            for (first, count), base in targets:
                at_col = c - first
                held = (at_col >= 0) & (at_col < count)
                tile = jnp.clip(at_col, 0, count - 1) // per_tile
                cols = pl.ds(pl.multiple_of(base + tile * LANES, LANES), LANES)
                from_lane = jnp.where(held, begin, LANES)
                pltpu.store(
                    ref.at[rows, cols], moved,
                    mask=(lane >= from_lane) & (lane < from_lane + vectors),
                )

        mine = blocks_ref[l, i, j]
        put(q, mine, 0)
        faces = ((ny, 0, i < nx - 1, i > 0), (1, 0, j < ny - 1, j > 0), (0, 1, l < nz - 1, l > 0))
        below = []
        lower = []
        for face, (dr, dl, up, down) in enumerate(faces):
            n = jnp.where(up, s + dr * nz + dl, s)
            put(jnp.where(up, slot_at(n), nowhere), mine, (face + 1) * vectors)
            n = jnp.where(down, s - dr * nz - dl, s)
            lower.append(jnp.where(down, slot_at(n), nowhere))
            r2, l2 = n // nz, n % nz
            below.append(pltpu.roll(blocks_ref[l2, r2 // ny, r2 % ny], LANES - (face + 1) * vectors, 1))
        turned = jnp.concatenate(below + [filler], axis=0).T[:vectors, :]
        for face in range(3):
            put(lower[face], turned, face * vectors)

    def top_row(q, carry):
        block_row(
            q, panel, q, (((0, wide), 0), (own_cols, width), (own_rows, width + cols_local))
        )
        return carry

    def own_row(n, carry):
        block_row(row_block + n, local, n, ((own_cols, 0),))
        return carry

    lax.fori_loop(0, wide, top_row, 0, unroll=4)
    lax.fori_loop(0, rows_local // vectors, own_row, 0, unroll=4)

    row = lax.broadcasted_iota(jnp.int32, (8, LANES), 0)
    groups = vectors // 8

    def times(left, right):
        return lax.dot_general(
            left, right, (((0,), (0,)), ((), ())), preferred_element_type=jnp.float32
        )

    for b in range(wide):
        begin = (b // per_tile) * LANES
        lane_at = (b % per_tile) * vectors
        body = [panel[b * vectors + 8 * g : b * vectors + 8 * g + 8, begin:] for g in range(groups)]
        tiles = body[0].shape[1] // LANES
        pivots, inverses = [], []
        for g in range(groups):
            pivot = jnp.ones((8, LANES), jnp.float32)
            inverse = pivot
            columns = [
                [
                    jnp.broadcast_to(
                        body[h][:, lane_at + 8 * g + t : lane_at + 8 * g + t + 1], (8, LANES)
                    )
                    for h in range(g, groups)
                ]
                for t in range(8)
            ]
            for t in range(8):
                head = columns[t][0][t : t + 1, :]
                turn = pl.reciprocal(head, approx=True)
                pivot = jnp.where(row == t, head, pivot)
                inverse = jnp.where(row == t, turn, inverse)
                kept = [jnp.where(row > t, columns[t][0], 0.0)] + columns[t][1:]
                for u in range(t + 1, 8):
                    across_row = columns[u][0][t : t + 1, :]
                    columns[u] = [
                        value - (part * across_row) * turn for value, part in zip(columns[u], kept)
                    ]
                body_row = body[g][t : t + 1, :]
                for h in range(g, groups):
                    factor = kept[h - g] * turn
                    body[h] = body[h] - jnp.concatenate([factor] * tiles, axis=1) * body_row
            pivots.append(pivot)
            inverses.append(inverse)
        strip = jnp.concatenate(body, axis=0)
        pivot = jnp.concatenate(pivots, axis=0)
        inverse = jnp.concatenate(inverses, axis=0)
        mine = strip[:, width + cols_local - begin :]
        across[b * vectors : (b + 1) * vectors, :] = mine * jnp.concatenate(
            [lax.rsqrt(pivot)] * (rows_local // LANES), axis=1
        )
        right = right_stack(strip)
        left_of = lambda value: left_stack(
            value * jnp.concatenate([inverse] * (value.shape[1] // LANES), axis=1)
        )
        for tile in range((b + 1) // per_tile, width // LANES):
            at = tile * LANES
            change = times(left_of(strip[:, at - begin : at - begin + LANES]), right[:, at - begin :])
            first = max((b + 1) * vectors, at)
            panel[first : at + LANES, at:] -= change[first - at :, :]
        local[...] -= times(left_of(mine), right[:, width - begin : width + cols_local - begin])

    row_ids = row_block * vectors + lax.broadcasted_iota(jnp.int32, (rows_local, LANES), 0)
    for tile in range(cols_local // LANES):
        at = slice(tile * LANES, (tile + 1) * LANES)
        start = iz * cols_local + tile * LANES
        col_ids = start + lax.broadcasted_iota(jnp.int32, (rows_local, LANES), 1)

        @pl.when(start < width)
        def _():
            part = across[pl.ds(pl.multiple_of(start, LANES), LANES), :]
            out_ref[:, at] = jnp.where(col_ids <= row_ids, part.T, 0.0)

        @pl.when(start >= width)
        def _():
            out_ref[:, at] = jnp.where(row_ids >= width, local[:, at], 0.0)


def on_device(probe_vectors, layer_ids, layer_kappa, slot_order):
    counts = tuple(lax.axis_size(axis) for axis in ("gx", "gy", "gz"))
    nx, ny, nz = counts
    vectors, ex, ey, ez = probe_vectors.shape
    layers = layer_kappa.shape[0]
    groups = vectors // 8
    vmem = pl.BlockSpec(memory_space=pltpu.VMEM)
    anywhere = pl.BlockSpec(memory_space=pltpu.HBM)
    phases = PASSES + 1
    dma = pltpu.SemaphoreType.DMA
    pinned = lambda value: pltpu.with_memory_space_constraint(value, pltpu.HBM)
    blocks = pl.pallas_call(
        functools.partial(basis_kernel, counts, (ex, ey, ez), vectors, layers),
        out_shape=jax.ShapeDtypeStruct((nz, nx, ny, vectors, LANES), jnp.float32),
        in_specs=[anywhere] * 3,
        out_specs=vmem,
        scratch_shapes=[
            pltpu.VMEM((vectors * ex * ey, ez), jnp.float32),
            pltpu.VMEM((ex, ey, ez), jnp.int32),
            pltpu.SMEM((layers,), jnp.float32),
            pltpu.VMEM((phases, ex + 2, ey + 2, groups + 1, 8, ez), jnp.float32),
            pltpu.VMEM((phases, groups + 1, 8, ez), jnp.float32),
            pltpu.VMEM((phases, 2, groups + 1, 8, ez), jnp.float32),
            pltpu.VMEM((groups, 8, ez), jnp.float32),
            pltpu.VMEM((7, ex * ey, 8, ez), jnp.float32),
            pltpu.VMEM((8, ez), jnp.float32),
            dma((3,)), dma((phases, 6)), dma((phases, 6)),
            dma((ny,)), dma((ny,)), dma((nz, ny)), dma((nz, ny)), dma((nx, nz, ny)), dma((nx, nz, ny)),
        ],
        compiler_params=pltpu.CompilerParams(
            collective_id=0, has_side_effects=True, vmem_limit_bytes=48 * 1024 * 1024
        ),
        name="basis",
    )(pinned(probe_vectors.reshape(vectors * ex * ey, ez)), pinned(layer_ids), pinned(layer_kappa))

    rows_local, cols_local = nz * vectors, nx * ny * vectors
    width = NPAN * min(PANEL, rows_local, cols_local)
    return pl.pallas_call(
        functools.partial(factor_kernel, counts, vectors, width, rows_local, cols_local),
        out_shape=jax.ShapeDtypeStruct((rows_local, cols_local), jnp.float32),
        in_specs=[anywhere, vmem],
        out_specs=vmem,
        scratch_shapes=[
            pltpu.SMEM((nz, nx * ny), jnp.int32),
            pltpu.SMEM((nx * ny * nz,), jnp.int32),
            pltpu.VMEM((width, width + cols_local + rows_local), jnp.float32),
            pltpu.VMEM((rows_local, cols_local), jnp.float32),
            pltpu.VMEM((width, rows_local), jnp.float32),
            dma(()),
        ],
        compiler_params=pltpu.CompilerParams(vmem_limit_bytes=48 * 1024 * 1024),
        name="factor",
    )(slot_order.T, blocks)


def solution(mesh):
    in_specs = (P(None, "gx", "gy", "gz"), P("gx", "gy", "gz"), P(), P())
    out_specs = P(("gx", "gy"), "gz")
    return jax.shard_map(
        on_device, mesh=mesh, in_specs=in_specs, out_specs=out_specs, check_vma=False
    )
```

```python
import functools
import math

import jax
import jax.numpy as jnp
from jax import lax
from jax.experimental import pallas as pl
from jax.experimental.pallas import tpu as pltpu
from jax.sharding import PartitionSpec as P

PASSES = 4
PANEL = 256
NPAN = 2
UPPER_EDGE = 120.0
LOWER_EDGE = 24.0
COARSE_SHIFT = 1.0
LANES = 128
MESH = pl.DeviceIdType.MESH


def cheb_factors(step_index):
    center = (UPPER_EDGE + LOWER_EDGE) / (UPPER_EDGE - LOWER_EDGE)
    growth = math.log(center + math.sqrt(center * center - 1.0))

    def chebval(degree):
        expo = math.exp(degree * growth)
        return 0.5 * (expo + 1.0 / expo)

    if step_index == 0:
        return (1.0 / chebval(1), 0.0)
    return (
        2.0 * chebval(step_index) / chebval(step_index + 1),
        chebval(step_index - 1) / chebval(step_index + 1),
    )


def basis_kernel(
    counts, extents, vectors, layers,
    probe_hbm, ids_hbm, kappa_hbm, out_ref,
    probe, ids, kappa_ref, field, zsend, zrecv, zghost, weight, weight_z,
    load_sem, send_sem, recv_sem, y_send, y_recv, z_send, z_recv, x_send, x_recv,
):
    nx, ny, nz = counts
    ex, ey, ez = extents
    groups = vectors // 8
    cells = ex * ey
    ix, iy, iz = lax.axis_index("gx"), lax.axis_index("gy"), lax.axis_index("gz")
    lines = (("gx", ix, nx), ("gy", iy, ny), ("gz", iz, nz))

    loads = [
        pltpu.make_async_copy(src, dst, load_sem.at[n])
        for n, (src, dst) in enumerate(((probe_hbm, probe), (ids_hbm, ids), (kappa_hbm, kappa_ref)))
    ]
    for load in loads:
        load.start()

    barrier = pltpu.get_barrier_semaphore()
    for axis, index, count in lines:
        for step in range(1, count):
            pl.semaphore_signal(
                barrier, inc=1, device_id={axis: lax.rem(index + step, count)}, device_id_type=MESH
            )

    lane = lax.broadcasted_iota(jnp.int32, (1, 8, ez), 2)
    even = lane % 2 == 0
    zero_plane = jnp.zeros((groups + 1, 8, ez), jnp.float32)
    inside = (ix > 0, ix < nx - 1, iy > 0, iy < ny - 1, iz > 0, iz < nz - 1)

    def clear(side, phase):
        if side < 2:
            for y in range(ey):
                field[phase, 0 if side == 0 else ex + 1, y + 1] = zero_plane
        elif side < 4:
            for x in range(ex):
                field[phase, x + 1, 0 if side == 2 else ey + 1] = zero_plane
        else:
            zrecv[phase, side - 4] = zero_plane

    for side in range(6):
        @pl.when(jnp.logical_not(inside[side]))
        def _():
            for phase in range(PASSES + 1):
                clear(side, phase)

    def number(x, y):
        return (x - 1) * ey + y - 1

    every = [(x, y) for y in range(1, ey + 1) for x in range(1, ex + 1)]
    order = [at for at in every if at[1] in (1, ey)] + [at for at in every if at[1] not in (1, ey)]
    edges = len([at for at in every if at[1] in (1, ey)])

    def copy_of(phase, side):
        span = pl.ds(0, groups + 1 if phase == 0 else groups)
        axis, index, _ = lines[side // 2]
        low = side % 2 == 0
        target = index - 1 if low else index + 1
        if side < 2:
            src = field.at[phase, 1 if low else ex, pl.ds(1, ey), span]
            dst = field.at[phase, ex + 1 if low else 0, pl.ds(1, ey), span]
        elif side < 4:
            src = field.at[phase, pl.ds(1, ex), 1 if low else ey, span]
            dst = field.at[phase, pl.ds(1, ex), ey + 1 if low else 0, span]
        else:
            src = zsend.at[phase, span]
            dst = zrecv.at[phase, 1 if low else 0, span]
        return pltpu.make_async_remote_copy(
            src_ref=src, dst_ref=dst,
            send_sem=send_sem.at[phase, side], recv_sem=recv_sem.at[phase, side],
            device_id={axis: target}, device_id_type=MESH,
        )

    def sides_of(phase, axis):
        return (2 * axis, 2 * axis + 1) if phase < PASSES else (2 * axis,)

    def send(phase, axis):
        for side in sides_of(phase, axis):
            @pl.when(inside[side])
            def _():
                copy_of(phase, side).start()

    def receive(phase, axis):
        for side in sides_of(phase, axis):
            @pl.when(inside[side ^ 1])
            def _():
                copy_of(phase, side).wait_recv()

    def packed(values, span):
        total = jnp.zeros((span, 8, ez), jnp.float32)
        for (x, y), value in values:
            k = number(x, y)
            turned = pltpu.roll(value, 2 * k, 2) if k else value
            total = jnp.where((lane == 2 * k) | (lane == (2 * k - 1) % ez), turned, total)
        return total

    def unpack(phase, span):
        above = pltpu.roll(zrecv[phase, 1, 0:span], ez - 1, 2)
        if phase == PASSES:
            return jnp.where(even, 0.0, above)
        return jnp.where(even, pltpu.roll(zrecv[phase, 0, 0:span], 1, 2), above)

    def ghost_of(value, k):
        return pltpu.roll(value, ez - 2 * k, 2) if k else value

    slope = 2.0 / (UPPER_EDGE - LOWER_EDGE)
    shift = (UPPER_EDGE + LOWER_EDGE) / (UPPER_EDGE - LOWER_EDGE)
    steps = ((1, 0), (-1, 0), (0, 1), (0, -1))

    def is_ghost(x, y, face):
        x2, y2 = x + steps[face][0], y + steps[face][1]
        return x2 in (0, ex + 1) or y2 in (0, ey + 1)

    def beside(phase, x, y, face):
        return field[phase, x + steps[face][0], y + steps[face][1], 0:groups]

    for load in loads:
        load.wait()
    for x, y in every:
        k = number(x, y)
        field[0, x, y, 0:groups] = probe[pl.ds(k, vectors, stride=cells), :].reshape(groups, 8, ez)
    for x in range(1, ex + 1):
        layer_of = ids[x - 1]
        kappa = jnp.zeros(layer_of.shape, jnp.float32)
        for layer in range(layers):
            kappa = jnp.where(layer_of == layer, kappa_ref[layer], kappa)
        for y in range(1, ey + 1):
            field[0, x, y, groups] = jnp.broadcast_to(kappa[y - 1 : y, :], (8, ez))

    pl.semaphore_wait(barrier, sum(count - 1 for _, _, count in lines))
    send(0, 1)
    zsend[0] = packed([((x, y), field[0, x, y]) for x, y in order], groups + 1)
    send(0, 2)
    send(0, 0)

    half = 0.5 * slope

    def kappa_at(x, y):
        return field[0, x, y, groups]

    def face_weight(x, y, face):
        weight[face, number(x, y)] = half * (
            kappa_at(x, y) + kappa_at(x + steps[face][0], y + steps[face][1])
        )

    flat = lane[0]
    for x, y in order:
        k = number(x, y)
        for face in range(4):
            if not is_ghost(x, y, face):
                face_weight(x, y, face)
        here = kappa_at(x, y)
        weight[4, k] = jnp.where(flat == ez - 1, 0.0, half * (here + pltpu.roll(here, ez - 1, 1)))
        weight[5, k] = jnp.where(flat == 0, 0.0, half * (here + pltpu.roll(here, 1, 1)))

    for phase in range(PASSES):
        factor_one, factor_two = cheb_factors(phase)
        for x, y in order:
            k = number(x, y)
            here = field[phase, x, y, 0:groups]
            value = shift * here
            for face in range(4):
                if not is_ghost(x, y, face):
                    value += weight[face, k][None] * (beside(phase, x, y, face) - here)
            value += weight[4, k][None] * (pltpu.roll(here, ez - 1, 2) - here)
            value += weight[5, k][None] * (pltpu.roll(here, 1, 2) - here)
            value = factor_one * value
            if phase > 0:
                value -= factor_two * field[phase - 1, x, y, 0:groups]
            field[phase + 1, x, y, 0:groups] = value
        for axis in range(3):
            receive(phase, axis)
        if phase == 0:
            ghosts = unpack(0, groups + 1)
            zsum = half * (zsend[0, groups] + ghosts[groups])
            weight_z[...] = jnp.where(even[0], 0.0, zsum)
            for x, y in order:
                k = number(x, y)
                for face in range(4):
                    if is_ghost(x, y, face):
                        face_weight(x, y, face)
                value = half * (kappa_at(x, y) + ghost_of(ghosts[groups:], k)[0])
                weight[6, k] = jnp.where((flat == 0) | (flat == ez - 1), value, 0.0)
        zghost[...] = unpack(phase, groups)
        done = []
        for n, (x, y) in enumerate(order):
            k = number(x, y)
            here = field[phase, x, y, 0:groups]
            value = weight[6, k][None] * (ghost_of(zghost[...], k) - here)
            for face in range(4):
                if is_ghost(x, y, face):
                    value += weight[face, k][None] * (beside(phase, x, y, face) - here)
            value = field[phase + 1, x, y, 0:groups] + factor_one * value
            field[phase + 1, x, y, 0:groups] = value
            if n == edges - 1:
                send(phase + 1, 1)
        send(phase + 1, 0)
        zsend[phase + 1, 0:groups] = packed(
            [((x, y), field[phase + 1, x, y, 0:groups]) for x, y in order], groups
        )
        send(phase + 1, 2)

    def product(left, right):
        left = jnp.concatenate(left, axis=1)
        right = jnp.concatenate(right, axis=1)
        left_high, right_high = left.astype(jnp.bfloat16), right.astype(jnp.bfloat16)
        left_low = (left - left_high.astype(jnp.float32)).astype(jnp.bfloat16)
        right_low = (right - right_high.astype(jnp.float32)).astype(jnp.bfloat16)
        return lax.dot_general(
            jnp.concatenate([left_high, left_high, left_low], axis=1),
            jnp.concatenate([right_high, right_low, right_high], axis=1),
            (((1,), (1,)), ((), ())), preferred_element_type=jnp.float32,
        )

    last = lambda x, y: field[PASSES, x, y, 0:groups].reshape(vectors, ez)
    images = []
    for x, y in every:
        k = number(x, y)
        here = field[PASSES, x, y, 0:groups]
        value = weight[6, k][None] * here
        for face in range(4):
            other = here if is_ghost(x, y, face) else here - beside(PASSES, x, y, face)
            value += weight[face, k][None] * other
        value += weight[4, k][None] * (here - pltpu.roll(here, ez - 1, 2))
        value += weight[5, k][None] * (here - pltpu.roll(here, 1, 2))
        images.append(value.reshape(vectors, ez))
    scale = 1.0 / (slope * math.sqrt(cells * ez))
    own = scale * product([last(x, y) for x, y in every], images)
    row = lax.broadcasted_iota(jnp.int32, own.shape, 0)
    column = lax.broadcasted_iota(jnp.int32, own.shape, 1)
    own += jnp.where(row == column, COARSE_SHIFT, 0.0)
    own = jnp.concatenate([own, jnp.zeros((vectors, LANES - vectors), jnp.float32)], axis=1)

    for axis in range(3):
        receive(PASSES, axis)
    zeros = jnp.zeros((vectors, ez), jnp.float32)

    def placed(value, face):
        rows = [zeros] * (LANES // vectors)
        rows[face + 1] = value.reshape(vectors, ez)
        return jnp.concatenate(rows, axis=0)

    left, right = [], []
    for y in range(1, ey + 1):
        left.append(last(ex, y))
        right.append(placed(weight[0, number(ex, y)][None] * beside(PASSES, ex, y, 0), 0))
    for x in range(1, ex + 1):
        left.append(last(x, ey))
        right.append(placed(weight[2, number(x, ey)][None] * beside(PASSES, x, ey, 2), 1))
    left.append(zsend[PASSES, 0:groups].reshape(vectors, ez))
    right.append(placed(weight_z[...][None] * unpack(PASSES, groups), 2))
    out_ref[iz, ix, iy] = own - scale * product(left, right)

    def spread(axis, index, count, source, sends, recvs, act):
        for step in range(1, count):
            chunk = out_ref.at[source]
            act(pltpu.make_async_remote_copy(
                src_ref=chunk, dst_ref=chunk, send_sem=sends(step), recv_sem=recvs(step),
                device_id={axis: lax.rem(index + step, count)}, device_id_type=MESH,
            ))

    def back(index, step, count):
        return lax.rem(index + count - step, count)

    def along_x(dz, dy, act):
        source = (back(iz, dz, nz), ix, back(iy, dy, ny))
        spread("gx", ix, nx, source, lambda step: x_send.at[step, dz, dy],
               lambda step: x_recv.at[step, dz, dy], act)

    def along_z(dy, act):
        source = (iz, ix, back(iy, dy, ny))
        spread("gz", iz, nz, source, lambda step: z_send.at[step, dy],
               lambda step: z_recv.at[step, dy], act)

    def along_y(act):
        spread("gy", iy, ny, (iz, ix, iy), lambda step: y_send.at[step],
               lambda step: y_recv.at[step], act)

    def arrived(source, send_at, recv_at, axis, index, count):
        chunk = out_ref.at[source]
        pltpu.make_async_remote_copy(
            src_ref=chunk, dst_ref=chunk, send_sem=send_at, recv_sem=recv_at,
            device_id={axis: lax.rem(index + 1, count)}, device_id_type=MESH,
        ).wait_recv()

    start = lambda copy: copy.start()
    along_y(start)
    along_z(0, start)
    along_x(0, 0, start)
    for dy in range(1, ny):
        arrived((iz, ix, back(iy, dy, ny)), y_send.at[dy], y_recv.at[dy], "gy", iy, ny)
        along_z(dy, start)
        along_x(0, dy, start)
    for dy in range(ny):
        for dz in range(1, nz):
            arrived((back(iz, dz, nz), ix, back(iy, dy, ny)), z_send.at[dz, dy], z_recv.at[dz, dy],
                    "gz", iz, nz)
            along_x(dz, dy, start)
    for dy in range(ny):
        for dz in range(nz):
            for dx in range(1, nx):
                arrived((back(iz, dz, nz), back(ix, dx, nx), back(iy, dy, ny)),
                        x_send.at[dx, dz, dy], x_recv.at[dx, dz, dy], "gx", ix, nx)

    finish = lambda copy: copy.wait_send()
    along_y(finish)
    for dy in range(ny):
        along_z(dy, finish)
        for dz in range(nz):
            along_x(dz, dy, finish)
    for phase in range(PASSES + 1):
        for axis in range(3):
            for side in sides_of(phase, axis):
                @pl.when(inside[side])
                def _():
                    copy_of(phase, side).wait_send()


def split(value):
    high = value.astype(jnp.bfloat16)
    rest = value - high.astype(jnp.float32)
    middle = rest.astype(jnp.bfloat16)
    return high, middle, (rest - middle.astype(jnp.float32)).astype(jnp.bfloat16)


def left_stack(value):
    high, middle, low = split(value)
    return jnp.concatenate([high, high, middle, high, low, middle], axis=0)


def right_stack(value):
    high, middle, low = split(value)
    return jnp.concatenate([high, middle, high, low, high, middle], axis=0)


def factor_kernel(
    counts, vectors, width, rows_local, cols_local,
    slots, blocks_ref, out_ref, place, strips, panel, local, across,
):
    nx, ny, nz = counts
    ix, iy, iz = lax.axis_index("gx"), lax.axis_index("gy"), lax.axis_index("gz")
    rows_total = nx * ny
    devices = rows_total * nz
    row_block = (ix * ny + iy) * (rows_local // vectors)
    wide = width // vectors
    per_tile = LANES // vectors
    own_cols = pl.ds(pl.multiple_of(iz * cols_local, LANES), cols_local)
    own_rows = pl.ds(pl.multiple_of(row_block * vectors, LANES), rows_local)

    def slot_at(s):
        return slots[s % nz, s // nz]

    def note(s, carry):
        place[slot_at(s)] = s
        return carry

    lax.fori_loop(0, devices, note, 0, unroll=8)
    lane = lax.broadcasted_iota(jnp.int32, (vectors, LANES), 1)
    filler = jnp.zeros((LANES - 3 * vectors, LANES), jnp.float32)

    def block_row(q, at):
        strip = strips.at[at]
        strip[...] = jnp.zeros(strip.shape, jnp.float32)
        s = place[q]
        r, l = s // nz, s % nz
        i, j = r // ny, r % ny

        def put(c, value, lane_at):
            cols = pl.ds(pl.multiple_of((c // per_tile) * LANES, LANES), LANES)
            begin = (c % per_tile) * vectors
            moved = pltpu.roll(value, lax.rem(begin + LANES - lane_at, LANES), 1)
            pltpu.store(
                strip.at[:, cols], moved, mask=(lane >= begin) & (lane < begin + vectors)
            )

        mine = blocks_ref[l, i, j]
        put(q, mine, 0)
        faces = ((ny, 0, i < nx - 1, i > 0), (1, 0, j < ny - 1, j > 0), (0, 1, l < nz - 1, l > 0))
        below = []
        lower = []
        for face, (dr, dl, up, down) in enumerate(faces):
            n = jnp.where(up, s + dr * nz + dl, s)
            put(jnp.where(up, slot_at(n), devices), mine, (face + 1) * vectors)
            n = jnp.where(down, s - dr * nz - dl, s)
            lower.append(jnp.where(down, slot_at(n), devices))
            r2, l2 = n // nz, n % nz
            below.append(pltpu.roll(blocks_ref[l2, r2 // ny, r2 % ny], LANES - (face + 1) * vectors, 1))
        turned = jnp.concatenate(below + [filler], axis=0).T[:vectors, :]
        for face in range(3):
            put(lower[face], turned, face * vectors)
        return strip

    def top_row(q, carry):
        strip = block_row(q, q % 4)
        rows = pl.ds(pl.multiple_of(q * vectors, vectors), vectors)
        panel[rows, :width] = strip[:, :width]
        panel[rows, width : width + cols_local] = strip[:, own_cols]
        panel[rows, width + cols_local :] = strip[:, own_rows]
        return carry

    def own_row(n, carry):
        strip = block_row(row_block + n, n % 4)
        rows = pl.ds(pl.multiple_of(n * vectors, vectors), vectors)
        local[rows, :] = strip[:, own_cols]
        return carry

    lax.fori_loop(0, wide, top_row, 0, unroll=4)
    lax.fori_loop(0, rows_local // vectors, own_row, 0, unroll=4)

    row = lax.broadcasted_iota(jnp.int32, (8, LANES), 0)
    groups = vectors // 8

    def times(left, right):
        return lax.dot_general(
            left, right, (((0,), (0,)), ((), ())), preferred_element_type=jnp.float32
        )

    for b in range(wide):
        begin = (b // per_tile) * LANES
        lane_at = (b % per_tile) * vectors
        body = [panel[b * vectors + 8 * g : b * vectors + 8 * g + 8, begin:] for g in range(groups)]
        tiles = body[0].shape[1] // LANES
        pivots, inverses = [], []
        for g in range(groups):
            pivot = jnp.ones((8, LANES), jnp.float32)
            inverse = pivot
            columns = [
                [
                    jnp.broadcast_to(
                        body[h][:, lane_at + 8 * g + t : lane_at + 8 * g + t + 1], (8, LANES)
                    )
                    for h in range(g, groups)
                ]
                for t in range(8)
            ]
            for t in range(8):
                head = columns[t][0][t : t + 1, :]
                turn = pl.reciprocal(head, approx=True)
                pivot = jnp.where(row == t, head, pivot)
                inverse = jnp.where(row == t, turn, inverse)
                kept = [jnp.where(row > t, columns[t][0], 0.0)] + columns[t][1:]
                for u in range(t + 1, 8):
                    across_row = columns[u][0][t : t + 1, :]
                    columns[u] = [
                        value - (part * across_row) * turn for value, part in zip(columns[u], kept)
                    ]
                body_row = body[g][t : t + 1, :]
                for h in range(g, groups):
                    factor = kept[h - g] * turn
                    body[h] = body[h] - jnp.concatenate([factor] * tiles, axis=1) * body_row
            pivots.append(pivot)
            inverses.append(inverse)
        strip = jnp.concatenate(body, axis=0)
        pivot = jnp.concatenate(pivots, axis=0)
        inverse = jnp.concatenate(inverses, axis=0)
        mine = strip[:, width + cols_local - begin :]
        across[b * vectors : (b + 1) * vectors, :] = mine * jnp.concatenate(
            [lax.rsqrt(pivot)] * (rows_local // LANES), axis=1
        )
        right = right_stack(strip)
        left_of = lambda value: left_stack(
            value * jnp.concatenate([inverse] * (value.shape[1] // LANES), axis=1)
        )
        for tile in range((b + 1) // per_tile, width // LANES):
            at = tile * LANES
            change = times(left_of(strip[:, at - begin : at - begin + LANES]), right[:, at - begin :])
            first = max((b + 1) * vectors, at)
            panel[first : at + LANES, at:] -= change[first - at :, :]
        local[...] -= times(left_of(mine), right[:, width - begin : width + cols_local - begin])

    row_ids = row_block * vectors + lax.broadcasted_iota(jnp.int32, (rows_local, LANES), 0)
    for tile in range(cols_local // LANES):
        at = slice(tile * LANES, (tile + 1) * LANES)
        start = iz * cols_local + tile * LANES
        col_ids = start + lax.broadcasted_iota(jnp.int32, (rows_local, LANES), 1)

        @pl.when(start < width)
        def _():
            part = across[pl.ds(pl.multiple_of(start, LANES), LANES), :]
            out_ref[:, at] = jnp.where(col_ids <= row_ids, part.T, 0.0)

        @pl.when(start >= width)
        def _():
            out_ref[:, at] = jnp.where(row_ids >= width, local[:, at], 0.0)


def on_device(probe_vectors, layer_ids, layer_kappa, slot_order):
    counts = tuple(lax.axis_size(axis) for axis in ("gx", "gy", "gz"))
    nx, ny, nz = counts
    vectors, ex, ey, ez = probe_vectors.shape
    layers = layer_kappa.shape[0]
    groups = vectors // 8
    vmem = pl.BlockSpec(memory_space=pltpu.VMEM)
    anywhere = pl.BlockSpec(memory_space=pltpu.HBM)
    phases = PASSES + 1
    dma = pltpu.SemaphoreType.DMA
    pinned = lambda value: pltpu.with_memory_space_constraint(value, pltpu.HBM)
    blocks = pl.pallas_call(
        functools.partial(basis_kernel, counts, (ex, ey, ez), vectors, layers),
        out_shape=jax.ShapeDtypeStruct((nz, nx, ny, vectors, LANES), jnp.float32),
        in_specs=[anywhere] * 3,
        out_specs=vmem,
        scratch_shapes=[
            pltpu.VMEM((vectors * ex * ey, ez), jnp.float32),
            pltpu.VMEM((ex, ey, ez), jnp.int32),
            pltpu.SMEM((layers,), jnp.float32),
            pltpu.VMEM((phases, ex + 2, ey + 2, groups + 1, 8, ez), jnp.float32),
            pltpu.VMEM((phases, groups + 1, 8, ez), jnp.float32),
            pltpu.VMEM((phases, 2, groups + 1, 8, ez), jnp.float32),
            pltpu.VMEM((groups, 8, ez), jnp.float32),
            pltpu.VMEM((7, ex * ey, 8, ez), jnp.float32),
            pltpu.VMEM((8, ez), jnp.float32),
            dma((3,)), dma((phases, 6)), dma((phases, 6)),
            dma((ny,)), dma((ny,)), dma((nz, ny)), dma((nz, ny)), dma((nx, nz, ny)), dma((nx, nz, ny)),
        ],
        compiler_params=pltpu.CompilerParams(
            collective_id=0, has_side_effects=True, vmem_limit_bytes=48 * 1024 * 1024
        ),
        name="basis",
    )(pinned(probe_vectors.reshape(vectors * ex * ey, ez)), pinned(layer_ids), pinned(layer_kappa))

    rows_local, cols_local = nz * vectors, nx * ny * vectors
    width = NPAN * min(PANEL, rows_local, cols_local)
    return pl.pallas_call(
        functools.partial(factor_kernel, counts, vectors, width, rows_local, cols_local),
        out_shape=jax.ShapeDtypeStruct((rows_local, cols_local), jnp.float32),
        in_specs=[pl.BlockSpec(memory_space=pltpu.SMEM), vmem],
        out_specs=vmem,
        scratch_shapes=[
            pltpu.SMEM((nx * ny * nz,), jnp.int32),
            pltpu.VMEM((4, vectors, nx * ny * nz * vectors + LANES), jnp.float32),
            pltpu.VMEM((width, width + cols_local + rows_local), jnp.float32),
            pltpu.VMEM((rows_local, cols_local), jnp.float32),
            pltpu.VMEM((width, rows_local), jnp.float32),
        ],
        compiler_params=pltpu.CompilerParams(vmem_limit_bytes=48 * 1024 * 1024),
        name="factor",
    )(slot_order.T, blocks)


def solution(mesh):
    in_specs = (P(None, "gx", "gy", "gz"), P("gx", "gy", "gz"), P(), P())
    out_specs = P(("gx", "gy"), "gz")
    return jax.shard_map(
        on_device, mesh=mesh, in_specs=in_specs, out_specs=out_specs, check_vma=False
    )
```
